32 devices in a mesh: role: 2 (over core), exp: 4 (over z), tp: 4 (over y, x).
Axes of the slice: x: 2, y: 2, z: 4, core: 2. Of those that a mesh axis runs over, the one named last changes fastest.
Arguments:
- residual_in: bfloat16 [256, 8192], P(('role', 'exp', 'tp')), may hold values from -64 to 64
- context: bfloat16 [256, 8192], P(('role', 'exp'), 'tp'), may hold values from -6 to 6
- out_weight: bfloat16 [8192, 8192], P('tp', ('role', 'exp')), may hold values from -0.0625 to 0.0625
- norm_gain: bfloat16 [8192], replicated, may hold values from 0.5 to 1.5
- router: bfloat16 [2, 4, 8192], replicated, may hold values from -0.125 to 0.125
- up_weight: bfloat16 [2, 4, 8192, 12288], P('role', 'exp', None, 'tp'), may hold values from -0.0625 to 0.0625
- down_weight: bfloat16 [2, 4, 12288, 8192], P('role', 'exp', 'tp'), may hold values from -0.109375 to 0.109375
- modality: int32 [256], P(('role', 'exp', 'tp')), may hold values from 0 to 1
- expert: int32 [256], P(('role', 'exp', 'tp')), may hold values from 0 to 3, as said below
Outputs:
- mixed: bfloat16 [256, 8192], P(('role', 'exp', 'tp'))
The draws below stay inside these ranges and needn't reach their ends.
Inputs may be any that keep to these rules, and one draw needn't show every extreme that they name: Among the 8 tokens of one device at most 2 choose one expert of one modality, and in every device's tokens some expert of some modality is chosen by exactly 2.
All inputs are finite; a program needn't handle non-finite values.
Results may differ from the reference program's by a relative error of at most 0.0052.
Values may be sent and summed in bfloat16 or wider, within the bound.
No kernel may reach another device: no remote copies, remote signals or barrier semaphores. Data moves between devices by JAX's collectives and lax.ppermute only.
A program may use at most 192 MiB of HBM per device.

```python
import jax
import jax.numpy as jnp
from jax import lax

D = 8192
FF = 12288
EXPERTS = 4
TOK_DEV = 8
CAP = 2
SPLIT = 1
TOKENS = 256


def route_table(key):
    base = jax.random.fold_in(key, 7)
    blocks = TOKENS // TOK_DEV
    pool_size = 2 * EXPERTS * CAP

    def one_block(block_key):
        kind_key, noise_key, favor_key, order_key = jax.random.split(block_key, 4)
        block_kind = jax.random.randint(kind_key, (), 0, 4)
        slot_ids = jnp.arange(pool_size, dtype=jnp.int32)
        composite = slot_ids // CAP
        modal_of = composite // EXPERTS
        favored = jax.random.randint(favor_key, (), 0, 2 * EXPERTS)
        noise_part = jax.random.randint(noise_key, (pool_size,), 0, 65536) * pool_size + slot_ids
        penalty = jnp.where(block_kind < 2, (modal_of == 0).astype(jnp.int32), jnp.where(block_kind == 2, (modal_of == 1).astype(jnp.int32), (composite != favored).astype(jnp.int32)))
        scores = noise_part + penalty * 16777216
        picked = composite[jnp.argsort(scores)[:TOK_DEV]]
        return picked[jax.random.permutation(order_key, TOK_DEV)]
    routed = jax.vmap(one_block)(jax.random.split(base, blocks))
    return routed.reshape(TOKENS).astype(jnp.int32)


def draw_modality(key, part):
    return (route_table(key) // EXPERTS).astype(jnp.int32)


def draw_expert(key, part):
    return (route_table(key) % EXPERTS).astype(jnp.int32)


def draw_residual_in(key, part):
    row_key, col_key, value_key = jax.random.split(jax.random.fold_in(key, 11), 3)
    row_scale = jnp.exp(jax.random.uniform(row_key, (TOKENS, 1), jnp.float32, -1.15, 1.15))
    col_scale = jnp.exp(jax.random.uniform(col_key, (1, D), jnp.float32, -1.15, 1.15))
    values = jnp.clip(jax.random.normal(value_key, (TOKENS, D), jnp.float32), -6.0, 6.0)
    return (values * row_scale * col_scale).astype(jnp.bfloat16)


def level_of(stream_key, dims, shards, least, high):
    gain, own = 1.0, jax.random.fold_in(stream_key, 6)
    for axis_at, blocks in shards:
        heights = jnp.exp(jax.random.uniform(jax.random.fold_in(own, axis_at), (blocks,), jnp.float32, least / len(shards), high / len(shards)))
        gain = gain * jnp.repeat(heights, dims[axis_at] // blocks).reshape([-1 if axis == axis_at else 1 for axis in range(len(dims))])
    return gain


def gaussian(rng, shape, deviation, limit, cuts=(), kind=jnp.bfloat16):
    level = level_of(rng, shape, cuts, -0.22, 0.18) if cuts else 1.0
    values = jax.random.normal(rng, shape, jnp.float32) * deviation * level
    return jnp.minimum(jnp.maximum(values, -limit), limit).astype(kind)


def setup_inputs(seed: int = 0) -> dict:
    keys = jax.random.split(jax.random.key(seed), 10)
    residual_in = draw_residual_in(jax.random.fold_in(keys[9], 71), 0)
    context = gaussian(keys[1], (TOKENS, D), 1.0, 6.0, ((0, 8), (1, 4)))
    out_weight = gaussian(keys[2], (D, D), D ** -0.5, 0.0625, ((0, 4), (1, 8)))
    norm_gain = jnp.clip(1.0 + 0.1 * jax.random.normal(keys[3], (D,), jnp.float32), 0.5, 1.5).astype(jnp.bfloat16)
    router = gaussian(keys[4], (2, EXPERTS, D), (D // 4) ** -0.5, 0.125)
    up_weight = gaussian(keys[5], (2, EXPERTS * SPLIT, D, FF // SPLIT), D ** -0.5, 0.0625, ((0, 2), (1, 4), (3, 4)))
    down_weight = gaussian(keys[6], (2, EXPERTS * SPLIT, FF // SPLIT, D), (FF // 4) ** -0.5, 0.109375, ((0, 2), (1, 4), (2, 4)))
    modality = draw_modality(jax.random.fold_in(keys[9], 71), 0)
    expert = draw_expert(jax.random.fold_in(keys[9], 71), 0)
    return dict(residual_in=residual_in, context=context, out_weight=out_weight, norm_gain=norm_gain, router=router, up_weight=up_weight, down_weight=down_weight, modality=modality, expert=expert)


EPSILON = 1e-05

def reference(residual_in, context, out_weight, norm_gain, router, up_weight, down_weight, modality, expert):
    projected = jnp.dot(context, out_weight, preferred_element_type=jnp.float32)
    resid = (residual_in.astype(jnp.float32) + projected).astype(jnp.bfloat16)
    resid = lax.optimization_barrier(resid)
    widened = resid.astype(jnp.float32)
    inverse_rms = lax.rsqrt(lax.optimization_barrier(jnp.mean(widened * widened, axis=-1, keepdims=True)) + EPSILON)
    normed = (widened * inverse_rms * norm_gain.astype(jnp.float32)).astype(jnp.bfloat16)
    routes = (modality * EXPERTS + expert).astype(jnp.int32)
    router_rows = router.reshape(2 * EXPERTS, D)
    picked = jnp.take(router_rows, routes, axis=0).astype(jnp.float32)
    gating = jax.nn.sigmoid(lax.optimization_barrier(jnp.sum(normed.astype(jnp.float32) * picked, axis=-1)))
    up_split = up_weight.reshape(2 * EXPERTS, SPLIT, D, FF // SPLIT)
    down_full = down_weight.reshape(2 * EXPERTS, FF, D)
    row_limit = TOKENS // 4

    def one_route(running, route_id):
        chosen = jnp.argsort((routes != route_id).astype(jnp.int32), stable=True)[:row_limit].astype(jnp.int32)
        matched = jnp.sum((routes == route_id).astype(jnp.int32))
        in_range = jnp.arange(row_limit, dtype=jnp.int32) < matched
        inputs = jnp.take(normed, chosen, axis=0)
        up_parts = lax.dynamic_index_in_dim(up_split, route_id, 0, keepdims=False)
        up_matrix = jnp.transpose(up_parts, (1, 0, 2)).reshape(D, FF)
        down_matrix = lax.dynamic_index_in_dim(down_full, route_id, 0, keepdims=False)
        up_sums = jnp.dot(inputs, up_matrix, preferred_element_type=jnp.float32)
        hidden = jax.nn.gelu(up_sums).astype(jnp.bfloat16)
        result = jnp.dot(hidden, down_matrix, preferred_element_type=jnp.float32)
        result = jnp.where(in_range[:, None], result, jnp.float32(0.0))
        return (running.at[chosen].add(result), None)
    summed, _ = lax.scan(one_route, jnp.zeros((TOKENS, D), jnp.float32), jnp.arange(2 * EXPERTS, dtype=jnp.int32))
    return (widened + gating[:, None] * summed).astype(jnp.bfloat16)
```

```python
import functools

import jax
import jax.numpy as jnp
from jax import lax
from jax.experimental import pallas as pl
from jax.experimental.pallas import tpu as pltpu
from jax.sharding import PartitionSpec as P

EXPERTS = 4
CAP = 2
EPSILON = 1e-05
MIB = 1 << 20
BF16 = jnp.bfloat16
F32 = jnp.float32

VMEM = pl.BlockSpec(memory_space=pltpu.VMEM)
SMEM = pl.BlockSpec(memory_space=pltpu.SMEM)
ANY = pl.BlockSpec(memory_space=pl.ANY)
HBM = pl.BlockSpec(memory_space=pltpu.HBM)


def swap(value, axis, distance):
    size = lax.axis_size(axis)
    return lax.ppermute(value, axis, [(i, i ^ distance) for i in range(size)])


def up_copies(step, exp_count, cols, place_ref, source_ref, out_ref, sems):
    copies = []
    for side in range(2):
        role = place_ref[0] if side == 0 else 1 - place_ref[0]
        start = pl.multiple_of((role * exp_count + (place_ref[1] ^ step)) * cols, cols)
        for part in range(4):
            size = cols // 4
            copies.append(
                pltpu.make_async_copy(
                    source_ref.at[pl.ds(pl.multiple_of(start + part * size, size), size)],
                    out_ref.at[pl.ds(side * cols + part * size, size)],
                    sems.at[4 * side + part],
                )
            )
    return copies


def fetch_kernel(step, exp_count, cols, place_ref, source_ref, *refs):
    out_ref, done_ref, sems = refs[-3:]
    copies = up_copies(step, exp_count, cols, place_ref, source_ref, out_ref, sems)
    for copy in copies:
        copy.start()
    done_ref[...] = jnp.zeros_like(done_ref)
    for copy in copies:
        copy.wait()


def fetch_up(step, exp_count, cols, lanes, place, matrix, after):
    units = matrix.shape[1]
    return pl.pallas_call(
        functools.partial(fetch_kernel, step, exp_count, cols),
        out_shape=[
            pltpu.VMEM((2 * cols, units), BF16),
            jax.ShapeDtypeStruct((8, lanes), BF16),
        ],
        in_specs=[SMEM, HBM] + [ANY] * len(after),
        out_specs=[VMEM] * 2,
        scratch_shapes=[pltpu.SemaphoreType.DMA((8,))],
        compiler_params=pltpu.CompilerParams(vmem_limit_bytes=MIB),
        cost_estimate=pl.CostEstimate(
            flops=0, bytes_accessed=4 * cols * units, transcendentals=0
        ),
        name="fetch_up",
    )(place, matrix, *after)


def project_kernel(tp_count, groups, place_ref, *refs):
    blocks, weight_ref = refs[:groups], refs[groups]
    outs, done_ref = refs[groups + 1 : -1], refs[-1]
    done_ref[...] = jnp.zeros_like(done_ref)
    tp_at = place_ref[2]
    tok_rows = blocks[0].shape[0] // tp_count
    cols = weight_ref.shape[1]
    rows = jnp.concatenate([block[...] for block in blocks], axis=0)
    tile = 256 if cols % 256 == 0 else cols
    for start in range(0, cols, tile):
        at_cols = slice(start, start + tile)
        sums = jnp.dot(rows, weight_ref[:, at_cols], preferred_element_type=F32)
        sums = sums.reshape(groups, tp_count, tok_rows, tile)
        for j in range(tp_count):
            wanted = tp_at ^ j
            block = sums[:, 0]
            for at in range(1, tp_count):
                block = jnp.where(wanted == at, sums[:, at], block)
            outs[j][:, at_cols] = block.reshape(groups * tok_rows, tile).astype(BF16)


def slot_kernel(tp_count, exp_count, split, place_ref, code_ref, residual_ref, *refs):
    parts, outs = refs[:tp_count], refs[tp_count:]
    role_at, exp_at = place_ref[0], place_ref[1]
    total = parts[0][...].astype(F32)
    for part in parts[1:]:
        total = total + part[...].astype(F32)
    resid = (residual_ref[...].astype(F32) + total).astype(BF16)
    count = resid.shape[0]
    slots = 2 * exp_count * CAP
    codes = code_ref[...]
    for out, role in zip(outs, (role_at, 1 - role_at)):
        for q in range(exp_count):
            route = role * EXPERTS + (exp_at ^ q) // split
            ids = lax.broadcasted_iota(jnp.int32, (slots, count), 0) + route * slots
            hot = (ids == codes).astype(F32).astype(BF16)
            picked = jnp.dot(hot, resid, preferred_element_type=F32)
            out[q] = picked.astype(BF16)


def lift(refs, first, place_ref, gain_ref, router_ref, split, exp_count, scaled, squares, logits):
    steps, _, slots, cols = refs[0].shape
    chosen = place_ref[1] // split
    for q in range(steps):
        for side in range(2):
            at = 2 * q + side
            role = place_ref[0] if side == 0 else 1 - place_ref[0]
            group = role * exp_count + (place_ref[1] ^ (first + q))
            at_cols = pl.ds(pl.multiple_of(group * cols, cols), cols)
            gain = gain_ref[:, at_cols]
            for j, ref in enumerate(refs):
                values = ref[q, side].astype(F32)
                squares[j] = squares[j] + jnp.sum(values * values, axis=1, keepdims=True)
                lifted = (values * gain).astype(BF16)
                scaled[j * slots : (j + 1) * slots, at * cols : (at + 1) * cols] = lifted
                if j == 0:
                    rows = router_ref[place_ref[0], :, at_cols].astype(F32)
                    rows_at = lax.broadcasted_iota(jnp.int32, rows.shape, 0)
                    weights = jnp.sum(jnp.where(rows_at == chosen, rows, 0.0), axis=0, keepdims=True)
                    logits = logits + jnp.sum(lifted.astype(F32) * weights, axis=1, keepdims=True)
    return squares, logits


def up_tile(units):
    return 256 if units % 256 == 0 else 128


def up_sums(scaled, up_refs, at_cols):
    total = None
    for at, ref in enumerate(up_refs):
        depth = ref.shape[0]
        term = jnp.dot(
            scaled[:, at * depth : (at + 1) * depth],
            ref[:, at_cols],
            preferred_element_type=F32,
        )
        total = term if total is None else total + term
    return total


def multiply(scaled, up_refs, last, copies, totals_ref, base, finish):
    units = totals_ref.shape[1]
    step = up_tile(units)
    cut = sum(ref.shape[0] for ref in up_refs)
    extra = scaled.shape[1] - cut

    @pl.loop(0, units // step)
    def _(at):
        at_cols = pl.ds(pl.multiple_of(at * step, step), step)
        sums = up_sums(scaled, up_refs, at_cols)
        totals_ref[:, at_cols] = sums if base is None else base[:, at_cols] + sums

    for copy in copies:
        copy.wait()
    if finish is not None:
        finish[0]()

    @pl.loop(0, units // step)
    def _(at):
        at_cols = pl.ds(pl.multiple_of(at * step, step), step)
        sums = totals_ref[:, at_cols]
        if extra:
            sums = sums + jnp.dot(scaled[:, cut:], last[:, at_cols], preferred_element_type=F32)
        if finish is None or finish[1] is None:
            totals_ref[:, at_cols] = sums
        else:
            finish[1](at_cols, sums)


def last_copies(first, count, exp_count, cols, place_ref, source_ref, last, sems):
    copies = []
    for at in range(count):
        copies += up_copies(
            first + at, exp_count, cols, place_ref, source_ref,
            last.at[pl.ds(at * 2 * cols, 2 * cols)], sems.at[at],
        )
    return copies


def first_kernel(sizes, place_ref, gain_ref, router_ref, *refs):
    tp_count, exp_count, split, near, ready = sizes
    rows_in, up_ref, source_ref = refs[:tp_count], refs[tp_count], refs[tp_count + 1]
    sums_ref, squares_ref, logits_ref = refs[tp_count + 2 : tp_count + 5]
    far_refs = refs[tp_count + 5 : tp_count + 5 + ready]
    scaled, last, last_sems, far_sems = refs[tp_count + 5 + ready :]
    slots, cols = rows_in[0].shape[2:]
    copies = last_copies(1, near - 1, exp_count, cols, place_ref, source_ref, last, last_sems)
    for copy in copies:
        copy.start()
    far_copies = []
    for at, far_ref in enumerate(far_refs):
        far_copies += up_copies(
            near + at, exp_count, cols, place_ref, source_ref, far_ref, far_sems.at[at]
        )
    zero = jnp.zeros((slots, 1), F32)
    squares, logits = lift(
        rows_in, 0, place_ref, gain_ref, router_ref, split, exp_count, scaled,
        [zero] * tp_count, zero,
    )
    squares_ref[...] = jnp.broadcast_to(jnp.concatenate(squares, axis=0), squares_ref.shape)
    logits_ref[...] = jnp.broadcast_to(logits, logits_ref.shape)

    def begin():
        for copy in far_copies:
            copy.start()

    multiply(scaled, [up_ref], last, copies, sums_ref, None, (begin, None))
    for copy in far_copies:
        copy.wait()


def down_loop(hidden, down_ref, outs, ring, sems, first, prime):
    depth, _, tile = ring.shape
    slots, width = outs[0].shape
    tiles = width // tile

    def fetch(at, slot):
        return pltpu.make_async_copy(
            down_ref.at[:, pl.ds(pl.multiple_of(first + at * tile, tile), tile)],
            ring.at[slot],
            sems.at[slot],
        )

    if prime:
        for at in range(min(depth, tiles)):
            fetch(at, at).start()
        return

    @pl.loop(0, tiles)
    def _(at):
        slot = lax.rem(at, depth)
        fetch(at, slot).wait()
        sums = jnp.dot(hidden[...], ring[slot], preferred_element_type=F32)
        at_cols = pl.ds(pl.multiple_of(at * tile, tile), tile)
        for j, out in enumerate(outs):
            out[:, at_cols] = sums[j * slots : (j + 1) * slots].astype(BF16)

        @pl.when(at + depth < tiles)
        def _():
            fetch(at + depth, slot).start()


def second_kernel(
    sizes, place_ref, gain_ref, router_ref, sums_ref, squares_ref, logits_ref, *refs
):
    tp_count, exp_count, split, near, far, width, early = sizes
    ready = far - far // 2
    rows_in, up_refs = refs[:tp_count], refs[tp_count : tp_count + ready]
    source_ref, down_ref = refs[tp_count + ready : tp_count + ready + 2]
    outs = refs[tp_count + ready + 2 : 2 * tp_count + ready + 2]
    hidden, gate_ref, held_ref, scaled, totals, last, last_sems, ring, sems, held_sem = refs[
        2 * tp_count + ready + 2 :
    ]
    slots, cols = rows_in[0].shape[2:]
    copies = last_copies(
        near + ready, far - ready, exp_count, cols, place_ref, source_ref, last, last_sems
    )
    for copy in copies:
        copy.start()
    held = pltpu.make_async_copy(
        down_ref.at[:, pl.ds(early, held_ref.shape[1])], held_ref, held_sem
    )
    squares = [squares_ref[j * slots : (j + 1) * slots, :1] for j in range(tp_count)]
    squares, logits = lift(
        rows_in, near, place_ref, gain_ref, router_ref, split, exp_count, scaled,
        squares, logits_ref[:, :1],
    )
    inverse = lax.rsqrt(jnp.concatenate(squares, axis=0) / width + EPSILON)
    gate_ref[...] = jnp.broadcast_to(jax.nn.sigmoid(logits * inverse[:slots]), gate_ref.shape)

    def begin():
        down_loop(hidden, down_ref, outs, ring, sems, 0, True)
        held.start()

    def end(at_cols, sums):
        hidden[:, at_cols] = jax.nn.gelu(sums * inverse).astype(BF16)

    multiply(scaled, up_refs, last, copies, totals, sums_ref, (begin, end))
    down_loop(hidden, down_ref, outs, ring, sems, 0, False)
    held.wait()


def third_kernel(tp_count, first, hidden, held_ref, down_ref, *refs):
    outs, (ring, sems) = refs[:tp_count], refs[tp_count:]
    slots = outs[0].shape[0]
    held = held_ref.shape[1]
    rest = [out.at[:, pl.ds(held, out.shape[1] - held)] for out in outs]
    down_loop(hidden, down_ref, rest, ring, sems, first + held, True)
    tile = ring.shape[2]

    @pl.loop(0, held // tile)
    def _(at):
        at_cols = pl.ds(pl.multiple_of(at * tile, tile), tile)
        sums = jnp.dot(hidden[...], held_ref[:, at_cols], preferred_element_type=F32)
        for j, out in enumerate(outs):
            out[:, at_cols] = sums[j * slots : (j + 1) * slots].astype(BF16)

    down_loop(hidden, down_ref, rest, ring, sems, first + held, False)


def combine_kernel(tp_count, exp_count, split, first, size, place_ref, rows_ref, gate_ref, *refs):
    summands, (stay_ref, leave_ref) = refs[:tp_count], refs[-2:]
    role_at, exp_at = place_ref[0], place_ref[1]
    cols = rows_ref.shape[3]
    count = stay_ref.shape[0]
    gate = gate_ref[:, :1]
    weight = jnp.where(exp_at % split == 0, 1.0, 0.0).astype(F32)
    for at in range(size // cols):
        group = first + at
        own = rows_ref[(group % exp_count) ^ exp_at, (group // exp_count) ^ role_at].astype(F32)
        at_cols = slice(at * cols, (at + 1) * cols)
        to_cols = slice(group * cols, (group + 1) * cols)
        total = summands[0][:, at_cols].astype(F32)
        for part in summands[1:]:
            total = total + part[:, at_cols].astype(F32)
        answers = own * weight + gate * total
        low, high = answers[:count], answers[count:]
        stay_ref[:, to_cols] = jnp.where(role_at == 0, low, high).astype(BF16)
        leave_ref[:, to_cols] = jnp.where(role_at == 0, high, low).astype(BF16)


def per_device(
    residual_in, context, out_weight, norm_gain, router, up_weight, down_weight, modality, expert
):
    tok_rows, width = residual_in.shape
    role_count, exp_count = lax.axis_size("role"), lax.axis_size("exp")
    tp_count = lax.axis_size("tp")
    role_at, exp_at, tp_at = (lax.axis_index(name) for name in ("role", "exp", "tp"))
    groups = role_count * exp_count
    split = exp_count // EXPERTS
    cols = out_weight.shape[1]
    slots = groups * CAP
    place = jnp.stack([role_at, exp_at, tp_at]).astype(jnp.int32)
    up_matrix, down_matrix = up_weight[0, 0], down_weight[0, 0]
    units = up_matrix.shape[1]
    in_hbm = lambda array: pltpu.with_memory_space_constraint(array, pltpu.HBM)
    up_matrix, down_matrix, out_weight = (in_hbm(a) for a in (up_matrix, down_matrix, out_weight))
    near_steps = exp_count // 2
    far_steps = exp_count - near_steps
    gains = norm_gain.astype(F32)[None, :]

    near = [context] + [swap(context, "exp", k) for k in range(1, exp_count)]

    routes = modality * EXPERTS + expert
    hot = (routes[:, None] == jnp.arange(2 * EXPERTS, dtype=jnp.int32)[None, :]).astype(jnp.int32)
    earlier = jnp.cumsum(hot, axis=0) - hot
    position = jnp.sum(earlier * hot, axis=1)
    code = routes * slots + (role_at * exp_count + exp_at) * CAP + position

    from_exp = (jnp.arange(exp_count) ^ exp_at) // split
    from_role = jnp.arange(2) ^ role_at
    row_route = (from_role[None, :] * EXPERTS + from_exp[:, None])[:, :, None]
    row_target = (row_route * CAP + jnp.arange(CAP)).reshape(-1)
    picks = ((routes * CAP + position)[:, None] == row_target[None, :]).astype(BF16)

    lanes = 128
    pieces = residual_in.reshape(tok_rows, role_count, exp_count, cols).transpose(1, 2, 0, 3)
    marks = jnp.broadcast_to(code.astype(BF16)[:, None], (role_count, exp_count, tok_rows, lanes))
    pieces = jnp.concatenate([pieces, marks], axis=3)
    mine = lax.dynamic_index_in_dim(pieces, role_at, 0, keepdims=False)
    other = lax.dynamic_index_in_dim(pieces, 1 - role_at, 0, keepdims=False)
    pair = jnp.stack([mine, swap(other, "role", 1)], axis=1)
    parted = [
        lax.dynamic_index_in_dim(pair, exp_at ^ k, 0, keepdims=False) for k in range(exp_count)
    ]

    up_block, done = fetch_up(
        0, exp_count, cols, context.shape[1], place, up_matrix, [*parted, gains, picks]
    )
    near[1:] = [
        (value.reshape(-1, *done.shape) + done).reshape(value.shape) for value in near[1:]
    ]
    blocks = []
    for value in near:
        blocks += [value, swap(value, "role", 1)]

    *partial_sums, done = pl.pallas_call(
        functools.partial(project_kernel, tp_count, groups),
        out_shape=[jax.ShapeDtypeStruct((groups * tok_rows, cols), BF16)] * tp_count
        + [jax.ShapeDtypeStruct((tok_rows, cols + lanes), BF16)],
        in_specs=[SMEM] + [VMEM] * (groups + 1),
        out_specs=[VMEM] * (tp_count + 1),
        compiler_params=pltpu.CompilerParams(vmem_limit_bytes=(8 if groups <= 8 else 24) * MIB),
        name="project",
    )(place, *blocks, out_weight)
    summands = [partial_sums[0]] + [swap(partial_sums[j], "tp", j) for j in range(1, tp_count)]

    gathered = [parted[0]] + [swap(parted[k] + done, "exp", k) for k in range(1, exp_count)]
    gathered = jnp.stack(gathered).reshape(groups * tok_rows, cols + lanes)
    residual_cols = gathered[:, :cols]
    codes = gathered[:, cols].astype(jnp.int32)[None, :]

    kept, leaving = pl.pallas_call(
        functools.partial(slot_kernel, tp_count, exp_count, split),
        out_shape=[jax.ShapeDtypeStruct((exp_count, slots, cols), BF16)] * 2,
        in_specs=[SMEM] + [VMEM] * (tp_count + 2),
        out_specs=[VMEM] * 2,
        compiler_params=pltpu.CompilerParams(vmem_limit_bytes=(6 if groups <= 8 else 24) * MIB),
        name="slot",
    )(place, codes, residual_cols, *summands)
    arrived = swap(leaving, "role", 1)
    routed = []
    for q in range(exp_count):
        both = jnp.stack([kept[q], arrived[q]])
        routed.append(swap(both, "exp", q) if q else both)
    near_rows = jnp.stack(routed[:near_steps])
    far_rows = jnp.stack(routed[near_steps:])
    near_all = [near_rows] + [swap(near_rows, "tp", j) for j in range(1, tp_count)]
    far_all = [far_rows] + [swap(far_rows, "tp", j) for j in range(1, tp_count)]

    rows = tp_count * slots
    small = rows <= 64
    half = near_steps * 2 * cols
    ready = far_steps - far_steps // 2
    in_vmem = lambda blocks: [pltpu.with_memory_space_constraint(b, pltpu.VMEM) for b in blocks]
    sums, squares, logits, *far_blocks = pl.pallas_call(
        functools.partial(first_kernel, (tp_count, exp_count, split, near_steps, ready)),
        out_shape=[
            pltpu.VMEM((rows, units), F32),
            pltpu.VMEM((rows, 128), F32),
            pltpu.VMEM((slots, 128), F32),
        ]
        + [pltpu.VMEM((2 * cols, units), BF16)] * ready,
        in_specs=[SMEM] + [VMEM] * (3 + tp_count) + [HBM],
        out_specs=[VMEM] * (3 + ready),
        scratch_shapes=[
            pltpu.VMEM((rows, half), BF16),
            pltpu.VMEM(((near_steps - 1) * 2 * cols, units), BF16),
            pltpu.SemaphoreType.DMA((near_steps - 1, 8)),
            pltpu.SemaphoreType.DMA((ready, 8)),
        ],
        compiler_params=pltpu.CompilerParams(vmem_limit_bytes=(21 if small else 36) * MIB),
        cost_estimate=pl.CostEstimate(
            flops=2 * rows * half * units, bytes_accessed=2 * half * units, transcendentals=0
        ),
        name="first",
    )(place, gains, router, *near_all, *in_vmem([up_block]), up_matrix)
    tile, depth = 256, 5
    early = width // 2
    held = early // tile // 4 * tile
    sizes = (tp_count, exp_count, split, near_steps, far_steps, width, early)
    *early_outs, hidden, gate, held_block = pl.pallas_call(
        functools.partial(second_kernel, sizes),
        out_shape=[jax.ShapeDtypeStruct((slots, early), BF16)] * tp_count
        + [jax.ShapeDtypeStruct((rows, units), BF16), jax.ShapeDtypeStruct((slots, 128), F32)]
        + [pltpu.VMEM((units, held), BF16)],
        in_specs=[SMEM] + [VMEM] * (5 + tp_count + ready) + [HBM] * 2,
        out_specs=[VMEM] * (tp_count + 3),
        scratch_shapes=[
            pltpu.VMEM((rows, width - half), BF16),
            pltpu.VMEM((rows, units), F32),
            pltpu.VMEM(((far_steps - ready) * 2 * cols, units), BF16),
            pltpu.SemaphoreType.DMA((far_steps - ready, 8)),
            pltpu.VMEM((depth, units, tile), BF16),
            pltpu.SemaphoreType.DMA((depth,)),
            pltpu.SemaphoreType.DMA,
        ],
        compiler_params=pltpu.CompilerParams(vmem_limit_bytes=(21 if small else 40) * MIB),
        cost_estimate=pl.CostEstimate(
            flops=4 * rows * half * units, bytes_accessed=4 * half * units, transcendentals=0
        ),
        name="second",
    )(
        place, gains, router, *in_vmem([sums, squares, logits]), *far_all, *in_vmem(far_blocks),
        up_matrix, down_matrix,
    )
    late_outs = pl.pallas_call(
        functools.partial(third_kernel, tp_count, early),
        out_shape=[jax.ShapeDtypeStruct((slots, width - early), BF16)] * tp_count,
        in_specs=[VMEM, VMEM, HBM],
        out_specs=[VMEM] * tp_count,
        scratch_shapes=[
            pltpu.VMEM((depth, units, tile), BF16),
            pltpu.SemaphoreType.DMA((depth,)),
        ],
        compiler_params=pltpu.CompilerParams(vmem_limit_bytes=(12 if small else 24) * MIB),
        cost_estimate=pl.CostEstimate(
            flops=2 * rows * half * units, bytes_accessed=2 * half * units, transcendentals=0
        ),
        name="third",
    )(hidden, *in_vmem([held_block]), down_matrix)

    early_sums = [early_outs[0]] + [swap(early_outs[j], "tp", j) for j in range(1, tp_count)]
    late_sums = [late_outs[0]] + [
        swap(late_outs[j] + 0 * early_sums[j], "tp", j) for j in range(1, tp_count)
    ]
    all_rows = jnp.concatenate([near_rows, far_rows])
    home = ()
    for start, summands in ((0, early_sums), (early, late_sums)):
        size = summands[0].shape[1]
        home = pl.pallas_call(
            functools.partial(
                combine_kernel, tp_count, exp_count, split, start // cols, size
            ),
            out_shape=[jax.ShapeDtypeStruct((exp_count * CAP, width), BF16)] * 2,
            in_specs=[SMEM] + [VMEM] * (tp_count + 2 + len(home)),
            out_specs=[VMEM] * 2,
            input_output_aliases={tp_count + 3 + at: at for at in range(len(home))},
            compiler_params=pltpu.CompilerParams(vmem_limit_bytes=(8 if small else 40) * MIB),
            name="combine",
        )(place, all_rows, gate, *summands, *home)
    stay, leave = home
    home = jnp.stack([stay, swap(leave, "role", 1)]).reshape(2, exp_count, CAP, width)
    returned = []
    for q in range(exp_count):
        piece = lax.dynamic_index_in_dim(home, exp_at ^ q, 1, keepdims=False)
        returned.append(swap(piece, "exp", q) if q else piece)
    returned = jnp.stack(returned).reshape(groups * CAP, width)
    return jnp.dot(picks, returned, preferred_element_type=F32).astype(BF16)


def solution(mesh):
    in_specs = (
        P(("role", "exp", "tp"), None),
        P(("role", "exp"), "tp"),
        P("tp", ("role", "exp")),
        P(),
        P(),
        P("role", "exp", None, "tp"),
        P("role", "exp", "tp", None),
        P(("role", "exp", "tp")),
        P(("role", "exp", "tp")),
    )
    out_specs = P(("role", "exp", "tp"), None)
    return jax.shard_map(
        per_device, mesh=mesh, in_specs=in_specs, out_specs=out_specs, check_vma=False
    )
```

```python
import functools

import jax
import jax.numpy as jnp
from jax import lax
from jax.experimental import pallas as pl
from jax.experimental.pallas import tpu as pltpu
from jax.sharding import PartitionSpec as P

EXPERTS = 4
CAP = 2
EPSILON = 1e-05
MIB = 1 << 20
BF16 = jnp.bfloat16
F32 = jnp.float32

VMEM = pl.BlockSpec(memory_space=pltpu.VMEM)
SMEM = pl.BlockSpec(memory_space=pltpu.SMEM)
ANY = pl.BlockSpec(memory_space=pl.ANY)
HBM = pl.BlockSpec(memory_space=pltpu.HBM)


def swap(value, axis, distance):
    size = lax.axis_size(axis)
    return lax.ppermute(value, axis, [(i, i ^ distance) for i in range(size)])


def up_copies(places, exp_count, cols, place_ref, source_ref, out_ref, sems):
    copies = []
    for at, (step, side) in enumerate(places):
        role = place_ref[0] if side == 0 else 1 - place_ref[0]
        start = pl.multiple_of((role * exp_count + (place_ref[1] ^ step)) * cols, cols)
        size = cols // 4
        for part in range(4):
            copies.append(
                pltpu.make_async_copy(
                    source_ref.at[pl.ds(pl.multiple_of(start + part * size, size), size)],
                    out_ref.at[pl.ds(at * cols + part * size, size)],
                    sems.at[4 * at + part],
                )
            )
    return copies


def fetch_kernel(places, exp_count, cols, place_ref, source_ref, *refs):
    out_ref, sems = refs[-2:]
    copies = up_copies(places, exp_count, cols, place_ref, source_ref, out_ref, sems)
    for copy in copies:
        copy.start()
    for copy in copies:
        copy.wait()


def fetch_up(places, exp_count, cols, place, matrix, after):
    units = matrix.shape[1]
    count = len(places)
    return pl.pallas_call(
        functools.partial(fetch_kernel, places, exp_count, cols),
        out_shape=pltpu.VMEM((count * cols, units), BF16),
        in_specs=[SMEM, HBM] + [ANY] * len(after),
        out_specs=VMEM,
        scratch_shapes=[pltpu.SemaphoreType.DMA((4 * count,))],
        compiler_params=pltpu.CompilerParams(vmem_limit_bytes=MIB),
        cost_estimate=pl.CostEstimate(
            flops=0, bytes_accessed=2 * count * cols * units, transcendentals=0
        ),
        name="fetch_up",
    )(place, matrix, *after)


def piece_kernel(exp_count, place_ref, residual_ref, codes_ref, *outs):
    role_at, exp_at = place_ref[0], place_ref[1]
    cols = outs[0].shape[2] - codes_ref.shape[1]
    for out, role in zip(outs, (role_at, 1 - role_at)):
        for q in range(exp_count):
            start = pl.multiple_of((role * exp_count + (exp_at ^ q)) * cols, cols)
            out[q, :, :cols] = residual_ref[:, pl.ds(start, cols)]
            out[q, :, cols:] = codes_ref[...]


def weight_kernel(source_ref, *refs):
    out_ref, done_ref, sems = refs[-3:]
    parts = sems.shape[0]
    size = source_ref.shape[0] // parts
    copies = [
        pltpu.make_async_copy(
            source_ref.at[pl.ds(at * size, size)], out_ref.at[pl.ds(at * size, size)], sems.at[at]
        )
        for at in range(parts)
    ]
    for copy in copies:
        copy.start()
    done_ref[...] = jnp.zeros_like(done_ref)
    for copy in copies:
        copy.wait()


def fetch_weight(matrix, after, lanes):
    return pl.pallas_call(
        weight_kernel,
        out_shape=[
            pltpu.VMEM(matrix.shape, matrix.dtype),
            jax.ShapeDtypeStruct((8, lanes), BF16),
        ],
        in_specs=[HBM] + [ANY] * len(after),
        out_specs=[VMEM] * 2,
        scratch_shapes=[pltpu.SemaphoreType.DMA((4,))],
        compiler_params=pltpu.CompilerParams(vmem_limit_bytes=MIB),
        cost_estimate=pl.CostEstimate(
            flops=0, bytes_accessed=2 * matrix.size, transcendentals=0
        ),
        name="fetch_weight",
    )(matrix, *after)


def project_kernel(tp_count, groups, place_ref, *refs):
    blocks, weight_ref = refs[:groups], refs[groups]
    outs = refs[groups + 1 :]
    tp_at = place_ref[2]
    tok_rows = blocks[0].shape[0] // tp_count
    cols = weight_ref.shape[1]
    rows = jnp.concatenate([block[...] for block in blocks], axis=0)
    tile = 256 if cols % 256 == 0 else cols
    for start in range(0, cols, tile):
        at_cols = slice(start, start + tile)
        sums = jnp.dot(rows, weight_ref[:, at_cols], preferred_element_type=F32)
        sums = sums.reshape(groups, tp_count, tok_rows, tile)
        for j in range(tp_count):
            wanted = tp_at ^ j
            block = sums[:, 0]
            for at in range(1, tp_count):
                block = jnp.where(wanted == at, sums[:, at], block)
            outs[j][:, at_cols] = block.reshape(groups * tok_rows, tile).astype(BF16)


def slot_kernel(tp_count, exp_count, split, steps, place_ref, code_ref, residual_ref, *refs):
    parts, outs = refs[:tp_count], refs[-2:]
    role_at, exp_at = place_ref[0], place_ref[1]
    total = parts[0][...].astype(F32)
    for part in parts[1:]:
        total = total + part[...].astype(F32)
    resid = (residual_ref[...].astype(F32) + total).astype(BF16)
    count = resid.shape[0]
    slots = 2 * exp_count * CAP
    codes = code_ref[...]
    at = lax.broadcasted_iota(jnp.int32, (slots, count), 0)
    side, away, place = at // (exp_count * CAP), at // CAP % exp_count, at % CAP
    for out, role in zip(outs, (role_at, 1 - role_at)):
        for to, q in enumerate(steps):
            exp_to = exp_at ^ q
            route = role * EXPERTS + exp_to // split
            group = (side ^ role) * exp_count + (away ^ exp_to)
            ids = route * slots + group * CAP + place
            hot = (ids == codes).astype(F32).astype(BF16)
            picked = jnp.dot(hot, resid, preferred_element_type=F32)
            out[to] = picked.astype(BF16)


def lift(refs, first, place_ref, gain_ref, router_ref, split, exp_count, scaled, squares, logits):
    steps, _, slots, cols = refs[0].shape
    chosen = place_ref[1] // split
    for q in range(steps):
        for side in range(2):
            at = 2 * q + side
            role = place_ref[0] if side == 0 else 1 - place_ref[0]
            group = role * exp_count + (place_ref[1] ^ (first + q))
            at_cols = pl.ds(pl.multiple_of(group * cols, cols), cols)
            gain = gain_ref[:, at_cols]
            for j, ref in enumerate(refs):
                values = ref[q, side].astype(F32)
                squares[j] = squares[j] + jnp.sum(values * values, axis=1, keepdims=True)
                lifted = (values * gain).astype(BF16)
                scaled[j * slots : (j + 1) * slots, at * cols : (at + 1) * cols] = lifted
                if j == 0:
                    rows = router_ref[place_ref[0], :, at_cols].astype(F32)
                    rows_at = lax.broadcasted_iota(jnp.int32, rows.shape, 0)
                    weights = jnp.sum(jnp.where(rows_at == chosen, rows, 0.0), axis=0, keepdims=True)
                    logits = logits + jnp.sum(lifted.astype(F32) * weights, axis=1, keepdims=True)
    return squares, logits


def up_tile(units, depth):
    step = units
    while step % 256 == 0 and step * depth > MIB * 3 // 2:
        step //= 2
    return step


def up_sums(scaled, up_refs, at_cols):
    total = None
    for at, ref in enumerate(up_refs):
        depth = ref.shape[0]
        term = jnp.dot(
            scaled[:, at * depth : (at + 1) * depth],
            ref[:, at_cols],
            preferred_element_type=F32,
        )
        total = term if total is None else total + term
    return total


def add_blocks(scaled, blocks, totals_ref, base, finish):
    units = totals_ref.shape[1]
    first = 0
    for number, (waits, block) in enumerate(blocks):
        for wait in waits:
            wait()
        depth = block.shape[0]
        step = up_tile(units, depth)
        rows = slice(first, first + depth)
        last = number == len(blocks) - 1

        @pl.loop(0, units // step)
        def _(at, number=number, block=block, rows=rows, last=last, step=step):
            at_cols = pl.ds(pl.multiple_of(at * step, step), step)
            sums = jnp.dot(scaled[:, rows], block[:, at_cols], preferred_element_type=F32)
            if number:
                sums = totals_ref[:, at_cols] + sums
            elif base is not None:
                sums = base[:, at_cols] + sums
            if last and finish is not None:
                finish(at_cols, sums)
            else:
                totals_ref[:, at_cols] = sums

        first += depth


def stream(places, exp_count, cols, place_ref, source_ref, blocks, sems):
    count, size, _ = blocks.shape
    copies = []
    for step, side in places:
        role = place_ref[0] if side == 0 else 1 - place_ref[0]
        start = (role * exp_count + (place_ref[1] ^ step)) * cols
        for part in range(cols // size):
            slot = len(copies) % count
            copies.append(
                pltpu.make_async_copy(
                    source_ref.at[pl.ds(pl.multiple_of(start + part * size, size), size)],
                    blocks.at[slot],
                    sems.at[slot],
                )
            )
    for copy in copies[:count]:
        copy.start()
    plan = []
    for at, copy in enumerate(copies):
        steps = [copy.wait]
        if 0 < at and at - 1 + count < len(copies):
            steps.insert(0, copies[at - 1 + count].start)
        plan.append((steps, blocks.at[at % count]))
    return plan


def first_kernel(sizes, place_ref, gain_ref, router_ref, up_ref, *refs):
    tp_count, exp_count, split, near = sizes
    rows_in, source_ref = refs[:tp_count], refs[tp_count]
    sums_ref, squares_ref, logits_ref, scaled, blocks, sems = refs[tp_count + 1 :]
    slots, cols = rows_in[0].shape[2:]
    places = [(q, side) for q in range(near) for side in range(2)][up_ref.shape[0] // cols :]
    plan = stream(places, exp_count, cols, place_ref, source_ref, blocks, sems)
    zero = jnp.zeros((slots, 1), F32)
    squares, logits = lift(
        rows_in, 0, place_ref, gain_ref, router_ref, split, exp_count, scaled,
        [zero] * tp_count, zero,
    )
    squares_ref[...] = jnp.broadcast_to(jnp.concatenate(squares, axis=0), squares_ref.shape)
    logits_ref[...] = jnp.broadcast_to(logits, logits_ref.shape)
    add_blocks(scaled, [([], up_ref)] + plan, sums_ref, None, None)


def down_loop(hidden, down_ref, outs, ring, sems, first, prime):
    depth, _, tile = ring.shape
    slots, width = outs[0].shape
    tiles = width // tile

    def fetch(at, slot):
        return pltpu.make_async_copy(
            down_ref.at[:, pl.ds(pl.multiple_of(first + at * tile, tile), tile)],
            ring.at[slot],
            sems.at[slot],
        )

    if prime:
        for at in range(min(depth, tiles)):
            fetch(at, at).start()
        return

    @pl.loop(0, tiles)
    def _(at):
        slot = lax.rem(at, depth)
        fetch(at, slot).wait()
        sums = jnp.dot(hidden[...], ring[slot], preferred_element_type=F32)
        at_cols = pl.ds(pl.multiple_of(at * tile, tile), tile)
        for j, out in enumerate(outs):
            out[:, at_cols] = sums[j * slots : (j + 1) * slots].astype(BF16)

        @pl.when(at + depth < tiles)
        def _():
            fetch(at + depth, slot).start()


def second_kernel(
    sizes, place_ref, gain_ref, router_ref, sums_ref, squares_ref, logits_ref, *refs
):
    tp_count, exp_count, split, near, far, width, early = sizes
    rows_in = refs[:tp_count]
    up_ref, source_ref, down_ref = refs[tp_count : tp_count + 3]
    outs = refs[tp_count + 3 : 2 * tp_count + 3]
    hidden, gate_ref, held_ref, scaled, totals, blocks, block_sems, ring, sems, held_sem = refs[
        2 * tp_count + 3 :
    ]
    slots, cols = rows_in[0].shape[2:]
    places = [(q, side) for q in range(near, near + far) for side in range(2)]
    places = places[up_ref.shape[0] // cols :]
    plan = stream(places, exp_count, cols, place_ref, source_ref, blocks, block_sems)
    last = max(1, len(plan) - blocks.shape[0] + 1)
    plan[min(last, len(plan) - 1)][0].insert(
        -1, lambda: down_loop(hidden, down_ref, outs, ring, sems, 0, True)
    )
    plan[-1][0].insert(-1, lambda: held.start())
    held = pltpu.make_async_copy(
        down_ref.at[:, pl.ds(early, held_ref.shape[1])], held_ref, held_sem
    )
    squares = [squares_ref[j * slots : (j + 1) * slots, :1] for j in range(tp_count)]
    squares, logits = lift(
        rows_in, near, place_ref, gain_ref, router_ref, split, exp_count, scaled,
        squares, logits_ref[:, :1],
    )
    inverse = lax.rsqrt(jnp.concatenate(squares, axis=0) / width + EPSILON)
    gate_ref[...] = jnp.broadcast_to(jax.nn.sigmoid(logits * inverse[:slots]), gate_ref.shape)

    def end(at_cols, sums):
        hidden[:, at_cols] = jax.nn.gelu(sums * inverse).astype(BF16)

    add_blocks(scaled, [([], up_ref)] + plan, totals, sums_ref, end)
    down_loop(hidden, down_ref, outs, ring, sems, 0, False)
    held.wait()


def third_kernel(tp_count, first, hidden, held_ref, down_ref, *refs):
    outs, (ring, sems) = refs[:tp_count], refs[tp_count:]
    slots = outs[0].shape[0]
    held = held_ref.shape[1]
    rest = [out.at[:, pl.ds(held, out.shape[1] - held)] for out in outs]
    down_loop(hidden, down_ref, rest, ring, sems, first + held, True)
    tile = ring.shape[2]

    @pl.loop(0, held // tile)
    def _(at):
        at_cols = pl.ds(pl.multiple_of(at * tile, tile), tile)
        sums = jnp.dot(hidden[...], held_ref[:, at_cols], preferred_element_type=F32)
        for j, out in enumerate(outs):
            out[:, at_cols] = sums[j * slots : (j + 1) * slots].astype(BF16)

    down_loop(hidden, down_ref, rest, ring, sems, first + held, False)


def combine_kernel(tp_count, exp_count, split, first, size, place_ref, rows_ref, gate_ref, *refs):
    summands, (stay_ref, leave_ref) = refs[:tp_count], refs[-2:]
    role_at, exp_at = place_ref[0], place_ref[1]
    cols = rows_ref.shape[3]
    count = stay_ref.shape[0]
    gate = gate_ref[:, :1]
    weight = jnp.where(exp_at % split == 0, 1.0, 0.0).astype(F32)
    for at in range(size // cols):
        group = first + at
        to_cols = slice(group * cols, (group + 1) * cols)
        own = rows_ref[(group % exp_count) ^ exp_at, (group // exp_count) ^ role_at].astype(F32)
        at_cols = slice(at * cols, (at + 1) * cols)
        total = summands[0][:, at_cols].astype(F32)
        for part in summands[1:]:
            total = total + part[:, at_cols].astype(F32)
        answers = own * weight + gate * total
        stay_ref[:, to_cols] = answers[:count].astype(BF16)
        leave_ref[:, to_cols] = answers[count:].astype(BF16)


def final_kernel(parts, picks_ref, *refs):
    pieces, out_ref = refs[:-1], refs[-1]
    picks = picks_ref[...].astype(F32)
    per_part = len(pieces) // parts
    first = 0
    for part in range(parts):
        size = pieces[part * per_part].shape[1]
        tile = 1024 if size % 1024 == 0 else size
        for start in range(0, size, tile):
            total, row_at = None, 0
            for piece in pieces[part * per_part : (part + 1) * per_part]:
                rows = piece[:, start : start + tile].astype(F32)
                for row in range(rows.shape[0]):
                    term = picks[:, row_at : row_at + 1] * rows[row : row + 1]
                    total = term if total is None else total + term
                    row_at += 1
            out_ref[:, first + start : first + start + tile] = total.astype(BF16)
        first += size


def per_device(
    residual_in, context, out_weight, norm_gain, router, up_weight, down_weight, modality, expert
):
    tok_rows, width = residual_in.shape
    role_count, exp_count = lax.axis_size("role"), lax.axis_size("exp")
    tp_count = lax.axis_size("tp")
    role_at, exp_at, tp_at = (lax.axis_index(name) for name in ("role", "exp", "tp"))
    groups = role_count * exp_count
    split = exp_count // EXPERTS
    cols = out_weight.shape[1]
    slots = groups * CAP
    place = jnp.stack([role_at, exp_at, tp_at]).astype(jnp.int32)
    up_matrix, down_matrix = up_weight[0, 0], down_weight[0, 0]
    units = up_matrix.shape[1]
    in_vmem = lambda blocks: [pltpu.with_memory_space_constraint(b, pltpu.VMEM) for b in blocks]
    in_hbm = lambda array: pltpu.with_memory_space_constraint(array, pltpu.HBM)
    up_matrix, down_matrix, out_weight = (in_hbm(a) for a in (up_matrix, down_matrix, out_weight))
    near_steps = exp_count // 2
    far_steps = exp_count - near_steps
    gains = norm_gain.astype(F32)[None, :]

    near = [context] + [swap(context, "exp", k) for k in range(1, exp_count)]

    routes = modality * EXPERTS + expert
    hot = (routes[:, None] == jnp.arange(2 * EXPERTS, dtype=jnp.int32)[None, :]).astype(jnp.int32)
    earlier = jnp.cumsum(hot, axis=0) - hot
    position = jnp.sum(earlier * hot, axis=1)
    code = routes * slots + (role_at * exp_count + exp_at) * CAP + position

    from_exp = (jnp.arange(exp_count) ^ exp_at) // split
    from_role = jnp.arange(2) ^ role_at
    row_route = (from_role[None, :] * EXPERTS + from_exp[:, None])[:, :, None]
    row_target = (row_route * CAP + jnp.arange(CAP)).reshape(-1)
    picks = ((routes * CAP + position)[:, None] == row_target[None, :]).astype(BF16)

    lanes = 128
    marks = jnp.broadcast_to(code.astype(BF16)[:, None], (tok_rows, lanes))
    mine, other = pl.pallas_call(
        functools.partial(piece_kernel, exp_count),
        out_shape=[jax.ShapeDtypeStruct((exp_count, tok_rows, cols + lanes), BF16)] * 2,
        in_specs=[SMEM] + [VMEM] * 2,
        out_specs=[VMEM] * 2,
        compiler_params=pltpu.CompilerParams(vmem_limit_bytes=4 * MIB),
        name="piece",
    )(place, residual_in, marks)
    head_cols = context.shape[1]
    zeros = max(head_cols, cols + lanes)
    weight, done = fetch_weight(out_weight, [place, other, gains, picks], zeros)
    arrived = swap(other, "role", 1) + done[:, : cols + lanes]
    parted = [jnp.stack([mine[k], arrived[k]]) for k in range(exp_count)]
    near[0] = (context.reshape(-1, 8, head_cols) + done[:, :head_cols]).reshape(context.shape)

    gathered = [parted[0]] + [swap(parted[k], "exp", k) for k in range(1, exp_count)]
    blocks = []
    for value in near:
        blocks += [value, swap(value if blocks else context, "role", 1)]

    partial_sums = pl.pallas_call(
        functools.partial(project_kernel, tp_count, groups),
        out_shape=[jax.ShapeDtypeStruct((groups * tok_rows, cols), BF16)] * tp_count,
        in_specs=[SMEM] + [VMEM] * (groups + 1),
        out_specs=[VMEM] * tp_count,
        compiler_params=pltpu.CompilerParams(vmem_limit_bytes=(8 if groups <= 8 else 24) * MIB),
        name="project",
    )(place, *blocks, in_vmem([weight])[0])
    summands = [partial_sums[0]] + [swap(partial_sums[j], "tp", j) for j in range(1, tp_count)]

    gathered = jnp.stack(gathered).reshape(groups * tok_rows, cols + lanes)
    residual_cols = gathered[:, :cols]
    codes = gathered[:, cols].astype(jnp.int32)[None, :]

    places = [(q, side) for q in range(exp_count) for side in range(2)]
    ahead = near_steps
    up_block = fetch_up(
        places[2 * near_steps : 2 * near_steps + ahead], exp_count, cols, place, up_matrix, [partial_sums[0], gains, picks]
    )

    routed, after = [], up_block
    for steps in (range(near_steps), range(near_steps, exp_count)):
        kept, leaving = pl.pallas_call(
            functools.partial(slot_kernel, tp_count, exp_count, split, steps),
            out_shape=[jax.ShapeDtypeStruct((len(steps), slots, cols), BF16)] * 2,
            in_specs=[SMEM] + [VMEM] * (tp_count + 2) + [ANY],
            out_specs=[VMEM] * 2,
            compiler_params=pltpu.CompilerParams(
                vmem_limit_bytes=(6 if groups <= 8 else 24) * MIB
            ),
            name="slot",
        )(place, codes, residual_cols, *summands, after)
        arrived = swap(leaving, "role", 1)
        for at, q in enumerate(steps):
            both = jnp.stack([kept[at], arrived[at]])
            routed.append(swap(both, "exp", q) if q else both)
            after = both
    near_rows = jnp.stack(routed[:near_steps])
    far_rows = jnp.stack(routed[near_steps:])
    near_block = fetch_up(places[:1], exp_count, cols, place, up_matrix, [near_rows])
    near_all = [near_rows] + [swap(near_rows, "tp", j) for j in range(1, tp_count)]
    far_all = [far_rows] + [swap(far_rows, "tp", j) for j in range(1, tp_count)]

    rows = tp_count * slots
    small = rows <= 64
    half = near_steps * 2 * cols
    sums, squares, logits = pl.pallas_call(
        functools.partial(first_kernel, (tp_count, exp_count, split, near_steps)),
        out_shape=[
            pltpu.VMEM((rows, units), F32),
            pltpu.VMEM((rows, 128), F32),
            pltpu.VMEM((slots, 128), F32),
        ],
        in_specs=[SMEM] + [VMEM] * (3 + tp_count) + [HBM],
        out_specs=[VMEM] * 3,
        scratch_shapes=[
            pltpu.VMEM((rows, half), BF16),
            pltpu.VMEM((4, cols // 2, units), BF16),
            pltpu.SemaphoreType.DMA((4,)),
        ],
        compiler_params=pltpu.CompilerParams(vmem_limit_bytes=(14 if small else 36) * MIB),
        cost_estimate=pl.CostEstimate(
            flops=2 * rows * half * units, bytes_accessed=2 * half * units, transcendentals=0
        ),
        name="first",
    )(place, gains, router, *in_vmem([near_block]), *near_all, up_matrix)
    tile, depth = 256, 4
    early = width // cols * 5 // 8 * cols
    held = width // tile // 8 * tile
    sizes = (tp_count, exp_count, split, near_steps, far_steps, width, early)
    *early_outs, hidden, gate, held_block = pl.pallas_call(
        functools.partial(second_kernel, sizes),
        out_shape=[jax.ShapeDtypeStruct((slots, early), BF16)] * tp_count
        + [jax.ShapeDtypeStruct((rows, units), BF16), jax.ShapeDtypeStruct((slots, 128), F32)]
        + [pltpu.VMEM((units, held), BF16)],
        in_specs=[SMEM] + [VMEM] * (6 + tp_count) + [HBM] * 2,
        out_specs=[VMEM] * (tp_count + 3),
        scratch_shapes=[
            pltpu.VMEM((rows, width - half), BF16),
            pltpu.VMEM((rows, units), F32),
            pltpu.VMEM((4, cols // 2, units), BF16),
            pltpu.SemaphoreType.DMA((4,)),
            pltpu.VMEM((depth, units, tile), BF16),
            pltpu.SemaphoreType.DMA((depth,)),
            pltpu.SemaphoreType.DMA,
        ],
        compiler_params=pltpu.CompilerParams(vmem_limit_bytes=(21 if small else 40) * MIB),
        cost_estimate=pl.CostEstimate(
            flops=4 * rows * half * units, bytes_accessed=4 * half * units, transcendentals=0
        ),
        name="second",
    )(
        place, gains, router, *in_vmem([sums, squares, logits]), *far_all, *in_vmem([up_block]),
        up_matrix, down_matrix,
    )
    late_outs = pl.pallas_call(
        functools.partial(third_kernel, tp_count, early),
        out_shape=[jax.ShapeDtypeStruct((slots, width - early), BF16)] * tp_count,
        in_specs=[VMEM, VMEM, HBM],
        out_specs=[VMEM] * tp_count,
        scratch_shapes=[
            pltpu.VMEM((depth, units, tile), BF16),
            pltpu.SemaphoreType.DMA((depth,)),
        ],
        compiler_params=pltpu.CompilerParams(vmem_limit_bytes=(12 if small else 24) * MIB),
        cost_estimate=pl.CostEstimate(
            flops=2 * rows * half * units, bytes_accessed=2 * half * units, transcendentals=0
        ),
        name="third",
    )(hidden, *in_vmem([held_block]), down_matrix)

    early_sums = [early_outs[0]] + [swap(early_outs[j], "tp", j) for j in range(1, tp_count)]
    late_sums = [late_outs[0]] + [
        swap(late_outs[j] + 0 * early_sums[j][:, : width - early], "tp", j) for j in range(1, tp_count)
    ]
    all_rows = jnp.concatenate([near_rows, far_rows])
    home = ()
    for start, summands in ((0, early_sums), (early, late_sums)):
        size = summands[0].shape[1]
        home = pl.pallas_call(
            functools.partial(
                combine_kernel, tp_count, exp_count, split, start // cols, size
            ),
            out_shape=[jax.ShapeDtypeStruct((exp_count * CAP, width), BF16)] * 2,
            in_specs=[SMEM] + [VMEM] * (tp_count + 2 + len(home)),
            out_specs=[VMEM] * 2,
            input_output_aliases={tp_count + 3 + at: at for at in range(len(home))},
            compiler_params=pltpu.CompilerParams(vmem_limit_bytes=(8 if small else 40) * MIB),
            name="combine",
        )(place, all_rows, gate, *summands, *home)
    stay, leave = home
    back = swap(leave, "role", 1)
    pieces = []
    for q in range(exp_count):
        own = slice(q * CAP, (q + 1) * CAP)
        piece = jnp.concatenate([stay[own], back[own]])
        pieces.append(swap(piece, "exp", q) if q else piece)
    return pl.pallas_call(
        functools.partial(final_kernel, 1),
        out_shape=jax.ShapeDtypeStruct((tok_rows, width), BF16),
        in_specs=[VMEM] * (1 + len(pieces)),
        out_specs=VMEM,
        compiler_params=pltpu.CompilerParams(vmem_limit_bytes=8 * MIB),
        name="final",
    )(picks, *pieces)


def solution(mesh):
    in_specs = (
        P(("role", "exp", "tp"), None),
        P(("role", "exp"), "tp"),
        P("tp", ("role", "exp")),
        P(),
        P(),
        P("role", "exp", None, "tp"),
        P("role", "exp", "tp", None),
        P(("role", "exp", "tp")),
        P(("role", "exp", "tp")),
    )
    out_specs = P(("role", "exp", "tp"), None)
    return jax.shard_map(
        per_device, mesh=mesh, in_specs=in_specs, out_specs=out_specs, check_vma=False
    )
```

```python
import functools

import jax
import jax.numpy as jnp
from jax import lax
from jax.experimental import pallas as pl
from jax.experimental.pallas import tpu as pltpu
from jax.sharding import PartitionSpec as P

EXPERTS = 4
CAP = 2
EPSILON = 1e-05
MIB = 1 << 20
BF16 = jnp.bfloat16
F32 = jnp.float32

VMEM = pl.BlockSpec(memory_space=pltpu.VMEM)
SMEM = pl.BlockSpec(memory_space=pltpu.SMEM)
ANY = pl.BlockSpec(memory_space=pl.ANY)
HBM = pl.BlockSpec(memory_space=pltpu.HBM)


def swap(value, axis, distance):
    size = lax.axis_size(axis)
    return lax.ppermute(value, axis, [(i, i ^ distance) for i in range(size)])


def up_copies(places, exp_count, cols, place_ref, source_ref, out_ref, sems):
    copies = []
    for at, (step, side) in enumerate(places):
        role = place_ref[0] if side == 0 else 1 - place_ref[0]
        start = pl.multiple_of((role * exp_count + (place_ref[1] ^ step)) * cols, cols)
        size = cols // 4
        for part in range(4):
            copies.append(
                pltpu.make_async_copy(
                    source_ref.at[pl.ds(pl.multiple_of(start + part * size, size), size)],
                    out_ref.at[pl.ds(at * cols + part * size, size)],
                    sems.at[4 * at + part],
                )
            )
    return copies


def fetch_kernel(places, exp_count, cols, place_ref, source_ref, *refs):
    out_ref, sems = refs[-2:]
    copies = up_copies(places, exp_count, cols, place_ref, source_ref, out_ref, sems)
    for copy in copies:
        copy.start()
    for copy in copies:
        copy.wait()


def fetch_up(places, exp_count, cols, place, matrix, after):
    units = matrix.shape[1]
    count = len(places)
    return pl.pallas_call(
        functools.partial(fetch_kernel, places, exp_count, cols),
        out_shape=pltpu.VMEM((count * cols, units), BF16),
        in_specs=[SMEM, HBM] + [ANY] * len(after),
        out_specs=VMEM,
        scratch_shapes=[pltpu.SemaphoreType.DMA((4 * count,))],
        compiler_params=pltpu.CompilerParams(vmem_limit_bytes=MIB),
        cost_estimate=pl.CostEstimate(
            flops=0, bytes_accessed=2 * count * cols * units, transcendentals=0
        ),
        name="fetch_up",
    )(place, matrix, *after)


def piece_kernel(exp_count, place_ref, residual_ref, codes_ref, *outs):
    role_at, exp_at = place_ref[0], place_ref[1]
    cols = outs[0].shape[2] - codes_ref.shape[1]
    for out, role in zip(outs, (role_at, 1 - role_at)):
        for q in range(exp_count):
            start = pl.multiple_of((role * exp_count + (exp_at ^ q)) * cols, cols)
            out[q, :, :cols] = residual_ref[:, pl.ds(start, cols)]
            out[q, :, cols:] = codes_ref[...]


def weight_kernel(source_ref, *refs):
    out_ref, done_ref, sems = refs[-3:]
    parts = sems.shape[0]
    size = source_ref.shape[0] // parts
    copies = [
        pltpu.make_async_copy(
            source_ref.at[pl.ds(at * size, size)], out_ref.at[pl.ds(at * size, size)], sems.at[at]
        )
        for at in range(parts)
    ]
    for copy in copies:
        copy.start()
    done_ref[...] = jnp.zeros_like(done_ref)
    for copy in copies:
        copy.wait()


def fetch_weight(matrix, after, lanes):
    return pl.pallas_call(
        weight_kernel,
        out_shape=[
            pltpu.VMEM(matrix.shape, matrix.dtype),
            jax.ShapeDtypeStruct((8, lanes), BF16),
        ],
        in_specs=[HBM] + [ANY] * len(after),
        out_specs=[VMEM] * 2,
        scratch_shapes=[pltpu.SemaphoreType.DMA((4,))],
        compiler_params=pltpu.CompilerParams(vmem_limit_bytes=MIB),
        cost_estimate=pl.CostEstimate(
            flops=0, bytes_accessed=2 * matrix.size, transcendentals=0
        ),
        name="fetch_weight",
    )(matrix, *after)


def project_kernel(tp_count, groups, place_ref, *refs):
    blocks, weight_ref = refs[:groups], refs[groups]
    outs = refs[groups + 1 :]
    tp_at = place_ref[2]
    tok_rows = blocks[0].shape[0] // tp_count
    cols = weight_ref.shape[1]
    rows = jnp.concatenate([block[...] for block in blocks], axis=0)
    tile = 256 if cols % 256 == 0 else cols
    for start in range(0, cols, tile):
        at_cols = slice(start, start + tile)
        sums = jnp.dot(rows, weight_ref[:, at_cols], preferred_element_type=F32)
        sums = sums.reshape(groups, tp_count, tok_rows, tile)
        for j in range(tp_count):
            wanted = tp_at ^ j
            block = sums[:, 0]
            for at in range(1, tp_count):
                block = jnp.where(wanted == at, sums[:, at], block)
            outs[j][:, at_cols] = block.reshape(groups * tok_rows, tile).astype(BF16)


def slot_kernel(tp_count, exp_count, split, steps, place_ref, code_ref, residual_ref, *refs):
    parts, outs = refs[:tp_count], refs[-2:]
    role_at, exp_at = place_ref[0], place_ref[1]
    total = parts[0][...].astype(F32)
    for part in parts[1:]:
        total = total + part[...].astype(F32)
    resid = (residual_ref[...].astype(F32) + total).astype(BF16)
    count = resid.shape[0]
    slots = 2 * exp_count * CAP
    codes = code_ref[...]
    at = lax.broadcasted_iota(jnp.int32, (slots, count), 0)
    side, away, place = at // (exp_count * CAP), at // CAP % exp_count, at % CAP
    for out, role in zip(outs, (role_at, 1 - role_at)):
        for to, q in enumerate(steps):
            exp_to = exp_at ^ q
            route = role * EXPERTS + exp_to // split
            group = (side ^ role) * exp_count + (away ^ exp_to)
            ids = route * slots + group * CAP + place
            hot = (ids == codes).astype(F32).astype(BF16)
            picked = jnp.dot(hot, resid, preferred_element_type=F32)
            out[to] = picked.astype(BF16)


def lift(refs, first, place_ref, gain_ref, router_ref, split, exp_count, scaled, squares, logits):
    steps, _, slots, cols = refs[0].shape
    chosen = place_ref[1] // split
    for q in range(steps):
        for side in range(2):
            at = 2 * q + side
            role = place_ref[0] if side == 0 else 1 - place_ref[0]
            group = role * exp_count + (place_ref[1] ^ (first + q))
            at_cols = pl.ds(pl.multiple_of(group * cols, cols), cols)
            gain = gain_ref[:, at_cols]
            for j, ref in enumerate(refs):
                values = ref[q, side].astype(F32)
                squares[j] = squares[j] + jnp.sum(values * values, axis=1, keepdims=True)
                lifted = (values * gain).astype(BF16)
                scaled[j * slots : (j + 1) * slots, at * cols : (at + 1) * cols] = lifted
                if j == 0:
                    rows = router_ref[place_ref[0], :, at_cols].astype(F32)
                    rows_at = lax.broadcasted_iota(jnp.int32, rows.shape, 0)
                    weights = jnp.sum(jnp.where(rows_at == chosen, rows, 0.0), axis=0, keepdims=True)
                    logits = logits + jnp.sum(lifted.astype(F32) * weights, axis=1, keepdims=True)
    return squares, logits


def up_tile(units, depth):
    widths = [n for n in range(256, units + 1, 256) if units % n == 0 and n * depth <= MIB * 3 // 2]
    return max(widths, default=128)


def up_sums(scaled, up_refs, at_cols):
    total = None
    for at, ref in enumerate(up_refs):
        depth = ref.shape[0]
        term = jnp.dot(
            scaled[:, at * depth : (at + 1) * depth],
            ref[:, at_cols],
            preferred_element_type=F32,
        )
        total = term if total is None else total + term
    return total


def add_blocks(scaled, blocks, totals_ref, base, finish):
    units = totals_ref.shape[1]
    first = 0
    for number, (waits, block) in enumerate(blocks):
        for wait in waits:
            wait()
        depth = block.shape[0]
        step = up_tile(units, depth)
        rows = slice(first, first + depth)
        last = number == len(blocks) - 1

        @pl.loop(0, units // step)
        def _(at, number=number, block=block, rows=rows, last=last, step=step):
            at_cols = pl.ds(pl.multiple_of(at * step, step), step)
            sums = jnp.dot(scaled[:, rows], block[:, at_cols], preferred_element_type=F32)
            if number:
                sums = totals_ref[:, at_cols] + sums
            elif base is not None:
                sums = base[:, at_cols] + sums
            if last and finish is not None:
                finish(at_cols, sums)
            else:
                totals_ref[:, at_cols] = sums

        first += depth


def stream(places, exp_count, cols, place_ref, source_ref, blocks, sems):
    count, size, _ = blocks.shape
    copies = []
    for step, side in places:
        role = place_ref[0] if side == 0 else 1 - place_ref[0]
        start = (role * exp_count + (place_ref[1] ^ step)) * cols
        for part in range(cols // size):
            slot = len(copies) % count
            copies.append(
                pltpu.make_async_copy(
                    source_ref.at[pl.ds(pl.multiple_of(start + part * size, size), size)],
                    blocks.at[slot],
                    sems.at[slot],
                )
            )
    for copy in copies[:count]:
        copy.start()
    plan = []
    for at, copy in enumerate(copies):
        steps = [copy.wait]
        if 0 < at and at - 1 + count < len(copies):
            steps.insert(0, copies[at - 1 + count].start)
        plan.append((steps, blocks.at[at % count]))
    return plan


def first_kernel(sizes, place_ref, gain_ref, router_ref, up_ref, *refs):
    tp_count, exp_count, split, near = sizes
    rows_in, source_ref = refs[:tp_count], refs[tp_count]
    sums_ref, squares_ref, logits_ref, scaled, blocks, sems = refs[tp_count + 1 :]
    slots, cols = rows_in[0].shape[2:]
    places = [(q, side) for q in range(near) for side in range(2)][up_ref.shape[0] // cols :]
    plan = stream(places, exp_count, cols, place_ref, source_ref, blocks, sems)
    zero = jnp.zeros((slots, 1), F32)
    squares, logits = lift(
        rows_in, 0, place_ref, gain_ref, router_ref, split, exp_count, scaled,
        [zero] * tp_count, zero,
    )
    squares_ref[...] = jnp.broadcast_to(jnp.concatenate(squares, axis=0), squares_ref.shape)
    logits_ref[...] = jnp.broadcast_to(logits, logits_ref.shape)
    add_blocks(scaled, [([], up_ref)] + plan, sums_ref, None, None)


def down_loop(hidden, down_ref, outs, ring, sems, first, prime):
    depth, _, tile = ring.shape
    slots, width = outs[0].shape
    tiles = width // tile

    def fetch(at, slot):
        return pltpu.make_async_copy(
            down_ref.at[:, pl.ds(pl.multiple_of(first + at * tile, tile), tile)],
            ring.at[slot],
            sems.at[slot],
        )

    if prime:
        for at in range(min(depth, tiles)):
            fetch(at, at).start()
        return

    @pl.loop(0, tiles)
    def _(at):
        slot = lax.rem(at, depth)
        fetch(at, slot).wait()
        sums = jnp.dot(hidden[...], ring[slot], preferred_element_type=F32)
        at_cols = pl.ds(pl.multiple_of(at * tile, tile), tile)
        for j, out in enumerate(outs):
            out[:, at_cols] = sums[j * slots : (j + 1) * slots].astype(BF16)

        @pl.when(at + depth < tiles)
        def _():
            fetch(at + depth, slot).start()


def second_kernel(
    sizes, place_ref, gain_ref, router_ref, sums_ref, squares_ref, logits_ref, *refs
):
    tp_count, exp_count, split, near, far, width, early = sizes
    rows_in = refs[:tp_count]
    up_ref, source_ref, down_ref = refs[tp_count : tp_count + 3]
    outs = refs[tp_count + 3 : 2 * tp_count + 3]
    hidden, gate_ref, held_ref, scaled, totals, blocks, block_sems, ring, sems, held_sem = refs[
        2 * tp_count + 3 :
    ]
    slots, cols = rows_in[0].shape[2:]
    places = [(q, side) for q in range(near, near + far) for side in range(2)]
    places = places[up_ref.shape[0] // cols :]
    plan = stream(places, exp_count, cols, place_ref, source_ref, blocks, block_sems)
    last = max(1, len(plan) - blocks.shape[0] + 1)
    plan[min(last, len(plan) - 1)][0].insert(
        -1, lambda: down_loop(hidden, down_ref, outs, ring, sems, 0, True)
    )
    plan[-1][0].insert(-1, lambda: held.start())
    held = pltpu.make_async_copy(
        down_ref.at[:, pl.ds(early, held_ref.shape[1])], held_ref, held_sem
    )
    squares = [squares_ref[j * slots : (j + 1) * slots, :1] for j in range(tp_count)]
    squares, logits = lift(
        rows_in, near, place_ref, gain_ref, router_ref, split, exp_count, scaled,
        squares, logits_ref[:, :1],
    )
    inverse = lax.rsqrt(jnp.concatenate(squares, axis=0) / width + EPSILON)
    gate_ref[...] = jnp.broadcast_to(jax.nn.sigmoid(logits * inverse[:slots]), gate_ref.shape)

    def end(at_cols, sums):
        hidden[:, at_cols] = jax.nn.gelu(sums * inverse).astype(BF16)

    add_blocks(scaled, [([], up_ref)] + plan, totals, sums_ref, end)
    down_loop(hidden, down_ref, outs, ring, sems, 0, False)
    held.wait()


def third_kernel(tp_count, first, hidden, held_ref, down_ref, *refs):
    outs, (ring, sems) = refs[:tp_count], refs[tp_count:]
    slots = outs[0].shape[0]
    held = held_ref.shape[1]
    rest = [out.at[:, pl.ds(held, out.shape[1] - held)] for out in outs]
    down_loop(hidden, down_ref, rest, ring, sems, first + held, True)
    tile = ring.shape[2]

    @pl.loop(0, held // tile)
    def _(at):
        at_cols = pl.ds(pl.multiple_of(at * tile, tile), tile)
        sums = jnp.dot(hidden[...], held_ref[:, at_cols], preferred_element_type=F32)
        for j, out in enumerate(outs):
            out[:, at_cols] = sums[j * slots : (j + 1) * slots].astype(BF16)

    down_loop(hidden, down_ref, rest, ring, sems, first + held, False)


def combine_kernel(tp_count, exp_count, split, first, size, place_ref, rows_ref, gate_ref, *refs):
    summands, (stay_ref, leave_ref) = refs[:tp_count], refs[-2:]
    role_at, exp_at = place_ref[0], place_ref[1]
    cols = rows_ref.shape[3]
    count = stay_ref.shape[0]
    gate = gate_ref[:, :1]
    weight = jnp.where(exp_at % split == 0, 1.0, 0.0).astype(F32)
    for at in range(size // cols):
        group = first + at
        to_cols = slice(group * cols, (group + 1) * cols)
        own = rows_ref[(group % exp_count) ^ exp_at, (group // exp_count) ^ role_at].astype(F32)
        at_cols = slice(at * cols, (at + 1) * cols)
        total = summands[0][:, at_cols].astype(F32)
        for part in summands[1:]:
            total = total + part[:, at_cols].astype(F32)
        answers = own * weight + gate * total
        stay_ref[:, to_cols] = answers[:count].astype(BF16)
        leave_ref[:, to_cols] = answers[count:].astype(BF16)


def final_kernel(picks_ref, *refs):
    pieces, out_ref = refs[:-1], refs[-1]
    picks = picks_ref[...]
    size = out_ref.shape[1]
    tile = 1024 if size % 1024 == 0 else size
    for start in range(0, size, tile):
        rows = jnp.concatenate(
            [piece[:, start : start + tile].astype(F32) for piece in pieces], axis=0
        )
        total = jnp.dot(picks, rows.astype(BF16), preferred_element_type=F32)
        out_ref[:, start : start + tile] = total.astype(BF16)


def per_device(
    residual_in, context, out_weight, norm_gain, router, up_weight, down_weight, modality, expert
):
    tok_rows, width = residual_in.shape
    role_count, exp_count = lax.axis_size("role"), lax.axis_size("exp")
    tp_count = lax.axis_size("tp")
    role_at, exp_at, tp_at = (lax.axis_index(name) for name in ("role", "exp", "tp"))
    groups = role_count * exp_count
    split = exp_count // EXPERTS
    cols = out_weight.shape[1]
    slots = groups * CAP
    place = jnp.stack([role_at, exp_at, tp_at]).astype(jnp.int32)
    up_matrix, down_matrix = up_weight[0, 0], down_weight[0, 0]
    units = up_matrix.shape[1]
    in_vmem = lambda blocks: [pltpu.with_memory_space_constraint(b, pltpu.VMEM) for b in blocks]
    in_hbm = lambda array: pltpu.with_memory_space_constraint(array, pltpu.HBM)
    up_matrix, down_matrix, out_weight = (in_hbm(a) for a in (up_matrix, down_matrix, out_weight))
    near_steps = exp_count // 2
    far_steps = exp_count - near_steps
    gains = norm_gain.astype(F32)[None, :]

    near = [context] + [swap(context, "exp", k) for k in range(1, exp_count)]

    routes = modality * EXPERTS + expert
    hot = (routes[:, None] == jnp.arange(2 * EXPERTS, dtype=jnp.int32)[None, :]).astype(jnp.int32)
    earlier = jnp.cumsum(hot, axis=0) - hot
    position = jnp.sum(earlier * hot, axis=1)
    code = routes * slots + (role_at * exp_count + exp_at) * CAP + position

    from_exp = (jnp.arange(exp_count) ^ exp_at) // split
    from_role = jnp.arange(2) ^ role_at
    row_route = (from_role[None, :] * EXPERTS + from_exp[:, None])[:, :, None]
    row_target = (row_route * CAP + jnp.arange(CAP)).reshape(-1)
    picks = ((routes * CAP + position)[:, None] == row_target[None, :]).astype(BF16)

    lanes = 128
    marks = jnp.broadcast_to(code.astype(BF16)[:, None], (tok_rows, lanes))
    mine, other = pl.pallas_call(
        functools.partial(piece_kernel, exp_count),
        out_shape=[jax.ShapeDtypeStruct((exp_count, tok_rows, cols + lanes), BF16)] * 2,
        in_specs=[SMEM] + [VMEM] * 2,
        out_specs=[VMEM] * 2,
        compiler_params=pltpu.CompilerParams(vmem_limit_bytes=4 * MIB),
        name="piece",
    )(place, residual_in, marks)
    head_cols = context.shape[1]
    zeros = max(head_cols, cols + lanes)
    weight, done = fetch_weight(out_weight, [place, other, gains, picks], zeros)
    arrived = swap(other, "role", 1) + done[:, : cols + lanes]
    parted = [jnp.stack([mine[k], arrived[k]]) for k in range(exp_count)]
    near[0] = (context.reshape(-1, 8, head_cols) + done[:, :head_cols]).reshape(context.shape)

    gathered = [parted[0]] + [swap(parted[k], "exp", k) for k in range(1, exp_count)]
    blocks = []
    for value in near:
        blocks += [value, swap(value if blocks else context, "role", 1)]

    partial_sums = pl.pallas_call(
        functools.partial(project_kernel, tp_count, groups),
        out_shape=[jax.ShapeDtypeStruct((groups * tok_rows, cols), BF16)] * tp_count,
        in_specs=[SMEM] + [VMEM] * (groups + 1),
        out_specs=[VMEM] * tp_count,
        compiler_params=pltpu.CompilerParams(vmem_limit_bytes=(8 if groups <= 8 else 24) * MIB),
        name="project",
    )(place, *blocks, in_vmem([weight])[0])
    summands = [partial_sums[0]] + [swap(partial_sums[j], "tp", j) for j in range(1, tp_count)]

    gathered = jnp.stack(gathered).reshape(groups * tok_rows, cols + lanes)
    residual_cols = gathered[:, :cols]
    codes = gathered[:, cols].astype(jnp.int32)[None, :]

    places = [(q, side) for q in range(exp_count) for side in range(2)]
    ahead = near_steps
    up_block = fetch_up(
        places[2 * near_steps : 2 * near_steps + ahead], exp_count, cols, place, up_matrix, [partial_sums[0], gains, picks]
    )

    routed, after = [], up_block
    for steps in (range(near_steps), range(near_steps, exp_count)):
        kept, leaving = pl.pallas_call(
            functools.partial(slot_kernel, tp_count, exp_count, split, steps),
            out_shape=[jax.ShapeDtypeStruct((len(steps), slots, cols), BF16)] * 2,
            in_specs=[SMEM] + [VMEM] * (tp_count + 2) + [ANY],
            out_specs=[VMEM] * 2,
            compiler_params=pltpu.CompilerParams(
                vmem_limit_bytes=(6 if groups <= 8 else 24) * MIB
            ),
            name="slot",
        )(place, codes, residual_cols, *summands, after)
        arrived = swap(leaving, "role", 1)
        for at, q in enumerate(steps):
            both = jnp.stack([kept[at], arrived[at]])
            routed.append(swap(both, "exp", q) if q else both)
            after = both
    near_rows = jnp.stack(routed[:near_steps])
    far_rows = jnp.stack(routed[near_steps:])
    near_block = fetch_up(places[:1], exp_count, cols, place, up_matrix, [near_rows])
    near_all = [near_rows] + [swap(near_rows, "tp", j) for j in range(1, tp_count)]
    far_all = [far_rows] + [swap(far_rows, "tp", j) for j in range(1, tp_count)]

    rows = tp_count * slots
    small = rows <= 64
    half = near_steps * 2 * cols
    sums, squares, logits = pl.pallas_call(
        functools.partial(first_kernel, (tp_count, exp_count, split, near_steps)),
        out_shape=[
            pltpu.VMEM((rows, units), F32),
            pltpu.VMEM((rows, 128), F32),
            pltpu.VMEM((slots, 128), F32),
        ],
        in_specs=[SMEM] + [VMEM] * (3 + tp_count) + [HBM],
        out_specs=[VMEM] * 3,
        scratch_shapes=[
            pltpu.VMEM((rows, half), BF16),
            pltpu.VMEM((4, cols // 2, units), BF16),
            pltpu.SemaphoreType.DMA((4,)),
        ],
        compiler_params=pltpu.CompilerParams(vmem_limit_bytes=(14 if small else 36) * MIB),
        cost_estimate=pl.CostEstimate(
            flops=2 * rows * half * units, bytes_accessed=2 * half * units, transcendentals=0
        ),
        name="first",
    )(place, gains, router, *in_vmem([near_block]), *near_all, up_matrix)
    tile, depth = 256, 4
    early = width // cols * 5 // 8 * cols
    held = width // tile // 8 * tile
    sizes = (tp_count, exp_count, split, near_steps, far_steps, width, early)
    *early_outs, hidden, gate, held_block = pl.pallas_call(
        functools.partial(second_kernel, sizes),
        out_shape=[jax.ShapeDtypeStruct((slots, early), BF16)] * tp_count
        + [jax.ShapeDtypeStruct((rows, units), BF16), jax.ShapeDtypeStruct((slots, 128), F32)]
        + [pltpu.VMEM((units, held), BF16)],
        in_specs=[SMEM] + [VMEM] * (6 + tp_count) + [HBM] * 2,
        out_specs=[VMEM] * (tp_count + 3),
        scratch_shapes=[
            pltpu.VMEM((rows, width - half), BF16),
            pltpu.VMEM((rows, units), F32),
            pltpu.VMEM((4, cols // 2, units), BF16),
            pltpu.SemaphoreType.DMA((4,)),
            pltpu.VMEM((depth, units, tile), BF16),
            pltpu.SemaphoreType.DMA((depth,)),
            pltpu.SemaphoreType.DMA,
        ],
        compiler_params=pltpu.CompilerParams(vmem_limit_bytes=(21 if small else 40) * MIB),
        cost_estimate=pl.CostEstimate(
            flops=4 * rows * half * units, bytes_accessed=4 * half * units, transcendentals=0
        ),
        name="second",
    )(
        place, gains, router, *in_vmem([sums, squares, logits]), *far_all, *in_vmem([up_block]),
        up_matrix, down_matrix,
    )
    late_outs = pl.pallas_call(
        functools.partial(third_kernel, tp_count, early),
        out_shape=[jax.ShapeDtypeStruct((slots, width - early), BF16)] * tp_count,
        in_specs=[VMEM, VMEM, HBM],
        out_specs=[VMEM] * tp_count,
        scratch_shapes=[
            pltpu.VMEM((depth, units, tile), BF16),
            pltpu.SemaphoreType.DMA((depth,)),
        ],
        compiler_params=pltpu.CompilerParams(vmem_limit_bytes=(12 if small else 24) * MIB),
        cost_estimate=pl.CostEstimate(
            flops=2 * rows * half * units, bytes_accessed=2 * half * units, transcendentals=0
        ),
        name="third",
    )(hidden, *in_vmem([held_block]), down_matrix)

    early_sums = [early_outs[0]] + [swap(early_outs[j], "tp", j) for j in range(1, tp_count)]
    late_sums = [late_outs[0]] + [
        swap(late_outs[j] + 0 * early_sums[j][:, : width - early], "tp", j) for j in range(1, tp_count)
    ]
    all_rows = jnp.concatenate([near_rows, far_rows])
    home = ()
    for start, summands in ((0, early_sums), (early, late_sums)):
        size = summands[0].shape[1]
        home = pl.pallas_call(
            functools.partial(
                combine_kernel, tp_count, exp_count, split, start // cols, size
            ),
            out_shape=[jax.ShapeDtypeStruct((exp_count * CAP, width), BF16)] * 2,
            in_specs=[SMEM] + [VMEM] * (tp_count + 2 + len(home)),
            out_specs=[VMEM] * 2,
            input_output_aliases={tp_count + 3 + at: at for at in range(len(home))},
            compiler_params=pltpu.CompilerParams(vmem_limit_bytes=(8 if small else 40) * MIB),
            name="combine",
        )(place, all_rows, gate, *summands, *home)
    stay, leave = home
    back = swap(leave, "role", 1)
    pieces = []
    for q in range(exp_count):
        own = slice(q * CAP, (q + 1) * CAP)
        piece = jnp.concatenate([stay[own], back[own]])
        pieces.append(swap(piece, "exp", q) if q else piece)
    return pl.pallas_call(
        final_kernel,
        out_shape=jax.ShapeDtypeStruct((tok_rows, width), BF16),
        in_specs=[VMEM] * (1 + len(pieces)),
        out_specs=VMEM,
        compiler_params=pltpu.CompilerParams(vmem_limit_bytes=8 * MIB),
        name="final",
    )(picks, *pieces)


def solution(mesh):
    in_specs = (
        P(("role", "exp", "tp"), None),
        P(("role", "exp"), "tp"),
        P("tp", ("role", "exp")),
        P(),
        P(),
        P("role", "exp", None, "tp"),
        P("role", "exp", "tp", None),
        P(("role", "exp", "tp")),
        P(("role", "exp", "tp")),
    )
    out_specs = P(("role", "exp", "tp"), None)
    return jax.shard_map(
        per_device, mesh=mesh, in_specs=in_specs, out_specs=out_specs, check_vma=False
    )
```

```python
import functools

import jax
import jax.numpy as jnp
from jax import lax
from jax.experimental import pallas as pl
from jax.experimental.pallas import tpu as pltpu
from jax.sharding import PartitionSpec as P

EXPERTS = 4
CAP = 2
EPSILON = 1e-05
MIB = 1 << 20
BF16 = jnp.bfloat16
F32 = jnp.float32

VMEM = pl.BlockSpec(memory_space=pltpu.VMEM)
SMEM = pl.BlockSpec(memory_space=pltpu.SMEM)
ANY = pl.BlockSpec(memory_space=pl.ANY)
HBM = pl.BlockSpec(memory_space=pltpu.HBM)


def swap(value, axis, distance):
    size = lax.axis_size(axis)
    return lax.ppermute(value, axis, [(i, i ^ distance) for i in range(size)])


def up_copies(places, exp_count, cols, place_ref, source_ref, out_ref, sems):
    copies = []
    for at, (step, side) in enumerate(places):
        role = place_ref[0] if side == 0 else 1 - place_ref[0]
        start = pl.multiple_of((role * exp_count + (place_ref[1] ^ step)) * cols, cols)
        size = cols // 4
        for part in range(4):
            copies.append(
                pltpu.make_async_copy(
                    source_ref.at[pl.ds(pl.multiple_of(start + part * size, size), size)],
                    out_ref.at[pl.ds(at * cols + part * size, size)],
                    sems.at[4 * at + part],
                )
            )
    return copies


def fetch_kernel(places, exp_count, cols, place_ref, source_ref, *refs):
    out_ref, sems = refs[-2:]
    copies = up_copies(places, exp_count, cols, place_ref, source_ref, out_ref, sems)
    for copy in copies:
        copy.start()
    for copy in copies:
        copy.wait()


def fetch_up(places, exp_count, cols, place, matrix, after):
    units = matrix.shape[1]
    count = len(places)
    return pl.pallas_call(
        functools.partial(fetch_kernel, places, exp_count, cols),
        out_shape=pltpu.VMEM((count * cols, units), BF16),
        in_specs=[SMEM, HBM] + [ANY] * len(after),
        out_specs=VMEM,
        scratch_shapes=[pltpu.SemaphoreType.DMA((4 * count,))],
        compiler_params=pltpu.CompilerParams(vmem_limit_bytes=MIB),
        cost_estimate=pl.CostEstimate(
            flops=0, bytes_accessed=2 * count * cols * units, transcendentals=0
        ),
        name="fetch_up",
    )(place, matrix, *after)


def piece_kernel(exp_count, place_ref, residual_ref, codes_ref, *outs):
    role_at, exp_at = place_ref[0], place_ref[1]
    cols = outs[0].shape[2] - codes_ref.shape[1]
    for out, role in zip(outs, (role_at, 1 - role_at)):
        for q in range(exp_count):
            start = pl.multiple_of((role * exp_count + (exp_at ^ q)) * cols, cols)
            out[q, :, :cols] = residual_ref[:, pl.ds(start, cols)]
            out[q, :, cols:] = codes_ref[...]


def weight_kernel(source_ref, *refs):
    out_ref, done_ref, sems = refs[-3:]
    parts = sems.shape[0]
    size = source_ref.shape[0] // parts
    copies = [
        pltpu.make_async_copy(
            source_ref.at[pl.ds(at * size, size)], out_ref.at[pl.ds(at * size, size)], sems.at[at]
        )
        for at in range(parts)
    ]
    for copy in copies:
        copy.start()
    done_ref[...] = jnp.zeros_like(done_ref)
    for copy in copies:
        copy.wait()


def fetch_weight(matrix, after, lanes):
    return pl.pallas_call(
        weight_kernel,
        out_shape=[
            pltpu.VMEM(matrix.shape, matrix.dtype),
            jax.ShapeDtypeStruct((8, lanes), BF16),
        ],
        in_specs=[HBM] + [ANY] * len(after),
        out_specs=[VMEM] * 2,
        scratch_shapes=[pltpu.SemaphoreType.DMA((4,))],
        compiler_params=pltpu.CompilerParams(vmem_limit_bytes=MIB),
        cost_estimate=pl.CostEstimate(
            flops=0, bytes_accessed=2 * matrix.size, transcendentals=0
        ),
        name="fetch_weight",
    )(matrix, *after)


def project_kernel(tp_count, groups, place_ref, *refs):
    blocks, weight_ref = refs[:groups], refs[groups]
    outs = refs[groups + 1 :]
    tp_at = place_ref[2]
    tok_rows = blocks[0].shape[0] // tp_count
    cols = weight_ref.shape[1]
    rows = jnp.concatenate([block[...] for block in blocks], axis=0)
    tile = 256 if cols % 256 == 0 else cols
    for start in range(0, cols, tile):
        at_cols = slice(start, start + tile)
        sums = jnp.dot(rows, weight_ref[:, at_cols], preferred_element_type=F32)
        sums = sums.reshape(groups, tp_count, tok_rows, tile)
        for j in range(tp_count):
            wanted = tp_at ^ j
            block = sums[:, 0]
            for at in range(1, tp_count):
                block = jnp.where(wanted == at, sums[:, at], block)
            outs[j][:, at_cols] = block.reshape(groups * tok_rows, tile).astype(BF16)


def slot_kernel(tp_count, exp_count, split, steps, place_ref, code_ref, residual_ref, *refs):
    parts, outs = refs[:tp_count], refs[-2:]
    role_at, exp_at = place_ref[0], place_ref[1]
    total = parts[0][...].astype(F32)
    for part in parts[1:]:
        total = total + part[...].astype(F32)
    resid = (residual_ref[...].astype(F32) + total).astype(BF16)
    count = resid.shape[0]
    slots = 2 * exp_count * CAP
    codes = code_ref[...]
    at = lax.broadcasted_iota(jnp.int32, (slots, count), 0)
    side, away, place = at // (exp_count * CAP), at // CAP % exp_count, at % CAP
    for out, role in zip(outs, (role_at, 1 - role_at)):
        for to, q in enumerate(steps):
            exp_to = exp_at ^ q
            route = role * EXPERTS + exp_to // split
            group = (side ^ role) * exp_count + (away ^ exp_to)
            ids = route * slots + group * CAP + place
            hot = (ids == codes).astype(F32).astype(BF16)
            picked = jnp.dot(hot, resid, preferred_element_type=F32)
            out[to] = picked.astype(BF16)


def lift(refs, first, place_ref, gain_ref, router_ref, split, exp_count, scaled, squares, logits):
    steps, _, slots, cols = refs[0].shape
    chosen = place_ref[1] // split
    for q in range(steps):
        for side in range(2):
            at = 2 * q + side
            role = place_ref[0] if side == 0 else 1 - place_ref[0]
            group = role * exp_count + (place_ref[1] ^ (first + q))
            at_cols = pl.ds(pl.multiple_of(group * cols, cols), cols)
            gain = gain_ref[:, at_cols]
            for j, ref in enumerate(refs):
                values = ref[q, side].astype(F32)
                squares[j] = squares[j] + jnp.sum(values * values, axis=1, keepdims=True)
                lifted = (values * gain).astype(BF16)
                scaled[j * slots : (j + 1) * slots, at * cols : (at + 1) * cols] = lifted
                if j == 0:
                    rows = router_ref[place_ref[0], :, at_cols].astype(F32)
                    rows_at = lax.broadcasted_iota(jnp.int32, rows.shape, 0)
                    weights = jnp.sum(jnp.where(rows_at == chosen, rows, 0.0), axis=0, keepdims=True)
                    logits = logits + jnp.sum(lifted.astype(F32) * weights, axis=1, keepdims=True)
    return squares, logits


def up_tile(units, depth):
    widths = [n for n in range(256, units + 1, 256) if units % n == 0 and n * depth <= MIB * 3 // 2]
    return max(widths, default=128)


def up_sums(scaled, up_refs, at_cols):
    total = None
    for at, ref in enumerate(up_refs):
        depth = ref.shape[0]
        term = jnp.dot(
            scaled[:, at * depth : (at + 1) * depth],
            ref[:, at_cols],
            preferred_element_type=F32,
        )
        total = term if total is None else total + term
    return total


def add_blocks(scaled, blocks, totals_ref, base, finish):
    units = totals_ref.shape[1]
    first = 0
    for number, (waits, block) in enumerate(blocks):
        for wait in waits:
            wait()
        depth = block.shape[0]
        step = up_tile(units, depth)
        rows = slice(first, first + depth)
        last = number == len(blocks) - 1

        @pl.loop(0, units // step)
        def _(at, number=number, block=block, rows=rows, last=last, step=step):
            at_cols = pl.ds(pl.multiple_of(at * step, step), step)
            sums = jnp.dot(scaled[:, rows], block[:, at_cols], preferred_element_type=F32)
            if number:
                sums = totals_ref[:, at_cols] + sums
            elif base is not None:
                sums = base[:, at_cols] + sums
            if last and finish is not None:
                finish(at_cols, sums)
            else:
                totals_ref[:, at_cols] = sums

        first += depth


def stream(places, exp_count, cols, place_ref, source_ref, blocks, sems):
    count, size, _ = blocks.shape
    copies = []
    for step, side in places:
        role = place_ref[0] if side == 0 else 1 - place_ref[0]
        start = (role * exp_count + (place_ref[1] ^ step)) * cols
        for part in range(cols // size):
            slot = len(copies) % count
            copies.append(
                pltpu.make_async_copy(
                    source_ref.at[pl.ds(pl.multiple_of(start + part * size, size), size)],
                    blocks.at[slot],
                    sems.at[slot],
                )
            )
    for copy in copies[:count]:
        copy.start()
    plan = []
    for at, copy in enumerate(copies):
        steps = [copy.wait]
        if 0 < at and at - 1 + count < len(copies):
            steps.insert(0, copies[at - 1 + count].start)
        plan.append((steps, blocks.at[at % count]))
    return plan


def first_kernel(sizes, place_ref, gain_ref, router_ref, up_ref, *refs):
    tp_count, exp_count, split, near = sizes
    rows_in, source_ref = refs[:tp_count], refs[tp_count]
    sums_ref, squares_ref, logits_ref, scaled, blocks, sems = refs[tp_count + 1 :]
    slots, cols = rows_in[0].shape[2:]
    places = [(q, side) for q in range(near) for side in range(2)][up_ref.shape[0] // cols :]
    plan = stream(places, exp_count, cols, place_ref, source_ref, blocks, sems)
    zero = jnp.zeros((slots, 1), F32)
    squares, logits = lift(
        rows_in, 0, place_ref, gain_ref, router_ref, split, exp_count, scaled,
        [zero] * tp_count, zero,
    )
    squares_ref[...] = jnp.broadcast_to(jnp.concatenate(squares, axis=0), squares_ref.shape)
    logits_ref[...] = jnp.broadcast_to(logits, logits_ref.shape)
    add_blocks(scaled, [([], up_ref)] + plan, sums_ref, None, None)


def down_loop(hidden, down_ref, outs, ring, sems, first, prime):
    depth, _, tile = ring.shape
    slots, width = outs[0].shape
    tiles = width // tile

    def fetch(at, slot):
        return pltpu.make_async_copy(
            down_ref.at[:, pl.ds(pl.multiple_of(first + at * tile, tile), tile)],
            ring.at[slot],
            sems.at[slot],
        )

    if prime:
        for at in range(min(depth, tiles)):
            fetch(at, at).start()
        return

    @pl.loop(0, tiles)
    def _(at):
        slot = lax.rem(at, depth)
        fetch(at, slot).wait()
        sums = jnp.dot(hidden[...], ring[slot], preferred_element_type=F32)
        at_cols = pl.ds(pl.multiple_of(at * tile, tile), tile)
        for j, out in enumerate(outs):
            out[:, at_cols] = sums[j * slots : (j + 1) * slots].astype(BF16)

        @pl.when(at + depth < tiles)
        def _():
            fetch(at + depth, slot).start()


def second_kernel(
    sizes, place_ref, gain_ref, router_ref, sums_ref, squares_ref, logits_ref, *refs
):
    tp_count, exp_count, split, near, far, width, early = sizes
    rows_in = refs[:tp_count]
    up_ref, source_ref, down_ref = refs[tp_count : tp_count + 3]
    outs = refs[tp_count + 3 : 2 * tp_count + 3]
    hidden, gate_ref, held_ref, scaled, totals, blocks, block_sems, ring, sems, held_sem = refs[
        2 * tp_count + 3 :
    ]
    slots, cols = rows_in[0].shape[2:]
    places = [(q, side) for q in range(near, near + far) for side in range(2)]
    places = places[up_ref.shape[0] // cols :]
    plan = stream(places, exp_count, cols, place_ref, source_ref, blocks, block_sems)
    last = max(1, len(plan) - blocks.shape[0] + 1)
    plan[min(last, len(plan) - 1)][0].insert(
        -1, lambda: down_loop(hidden, down_ref, outs, ring, sems, 0, True)
    )
    plan[-1][0].insert(-1, lambda: held.start())
    held = pltpu.make_async_copy(
        down_ref.at[:, pl.ds(early, held_ref.shape[1])], held_ref, held_sem
    )
    squares = [squares_ref[j * slots : (j + 1) * slots, :1] for j in range(tp_count)]
    squares, logits = lift(
        rows_in, near, place_ref, gain_ref, router_ref, split, exp_count, scaled,
        squares, logits_ref[:, :1],
    )
    inverse = lax.rsqrt(jnp.concatenate(squares, axis=0) / width + EPSILON)
    gate_ref[...] = jnp.broadcast_to(jax.nn.sigmoid(logits * inverse[:slots]), gate_ref.shape)

    def end(at_cols, sums):
        hidden[:, at_cols] = jax.nn.gelu(sums * inverse).astype(BF16)

    add_blocks(scaled, [([], up_ref)] + plan, totals, sums_ref, end)
    down_loop(hidden, down_ref, outs, ring, sems, 0, False)
    held.wait()


def third_kernel(tp_count, first, hidden, held_ref, down_ref, *refs):
    outs, (ring, sems) = refs[:tp_count], refs[tp_count:]
    slots = outs[0].shape[0]
    held = held_ref.shape[1]
    rest = [out.at[:, pl.ds(held, out.shape[1] - held)] for out in outs]
    down_loop(hidden, down_ref, rest, ring, sems, first + held, True)
    tile = ring.shape[2]

    @pl.loop(0, held // tile)
    def _(at):
        at_cols = pl.ds(pl.multiple_of(at * tile, tile), tile)
        sums = jnp.dot(hidden[...], held_ref[:, at_cols], preferred_element_type=F32)
        for j, out in enumerate(outs):
            out[:, at_cols] = sums[j * slots : (j + 1) * slots].astype(BF16)

    down_loop(hidden, down_ref, rest, ring, sems, first + held, False)


def combine_kernel(tp_count, exp_count, split, first, size, place_ref, rows_ref, gate_ref, *refs):
    summands, (stay_ref, leave_ref) = refs[:tp_count], refs[-2:]
    role_at, exp_at = place_ref[0], place_ref[1]
    cols = rows_ref.shape[3]
    count = stay_ref.shape[0]
    gate = gate_ref[:, :1]
    weight = jnp.where(exp_at % split == 0, 1.0, 0.0).astype(F32)
    for at in range(size // cols):
        group = first + at
        to_cols = slice(group * cols, (group + 1) * cols)
        own = rows_ref[(group % exp_count) ^ exp_at, (group // exp_count) ^ role_at].astype(F32)
        at_cols = slice(at * cols, (at + 1) * cols)
        total = summands[0][:, at_cols].astype(F32)
        for part in summands[1:]:
            total = total + part[:, at_cols].astype(F32)
        answers = own * weight + gate * total
        stay_ref[:, to_cols] = answers[:count].astype(BF16)
        leave_ref[:, to_cols] = answers[count:].astype(BF16)


def final_kernel(picks_ref, *refs):
    pieces, out_ref = refs[:-1], refs[-1]
    picks = picks_ref[...]
    size = out_ref.shape[1]
    tile = 1024 if size % 1024 == 0 else size
    for start in range(0, size, tile):
        rows = jnp.concatenate(
            [piece[:, start : start + tile].astype(F32) for piece in pieces], axis=0
        )
        total = jnp.dot(picks, rows.astype(BF16), preferred_element_type=F32)
        out_ref[:, start : start + tile] = total.astype(BF16)


def per_device(
    residual_in, context, out_weight, norm_gain, router, up_weight, down_weight, modality, expert
):
    tok_rows, width = residual_in.shape
    role_count, exp_count = lax.axis_size("role"), lax.axis_size("exp")
    tp_count = lax.axis_size("tp")
    role_at, exp_at, tp_at = (lax.axis_index(name) for name in ("role", "exp", "tp"))
    groups = role_count * exp_count
    split = exp_count // EXPERTS
    cols = out_weight.shape[1]
    slots = groups * CAP
    place = jnp.stack([role_at, exp_at, tp_at]).astype(jnp.int32)
    up_matrix, down_matrix = up_weight[0, 0], down_weight[0, 0]
    units = up_matrix.shape[1]
    in_vmem = lambda blocks: [pltpu.with_memory_space_constraint(b, pltpu.VMEM) for b in blocks]
    in_hbm = lambda array: pltpu.with_memory_space_constraint(array, pltpu.HBM)
    up_matrix, down_matrix, out_weight = (in_hbm(a) for a in (up_matrix, down_matrix, out_weight))
    near_steps = exp_count // 2
    far_steps = exp_count - near_steps
    gains = norm_gain.astype(F32)[None, :]

    near = [context] + [swap(context, "exp", k) for k in range(1, exp_count)]

    routes = modality * EXPERTS + expert
    hot = (routes[:, None] == jnp.arange(2 * EXPERTS, dtype=jnp.int32)[None, :]).astype(jnp.int32)
    earlier = jnp.cumsum(hot, axis=0) - hot
    position = jnp.sum(earlier * hot, axis=1)
    code = routes * slots + (role_at * exp_count + exp_at) * CAP + position

    from_exp = (jnp.arange(exp_count) ^ exp_at) // split
    from_role = jnp.arange(2) ^ role_at
    row_route = (from_role[None, :] * EXPERTS + from_exp[:, None])[:, :, None]
    row_target = (row_route * CAP + jnp.arange(CAP)).reshape(-1)
    picks = ((routes * CAP + position)[:, None] == row_target[None, :]).astype(BF16)

    lanes = 128
    marks = jnp.broadcast_to(code.astype(BF16)[:, None], (tok_rows, lanes))
    mine, other = pl.pallas_call(
        functools.partial(piece_kernel, exp_count),
        out_shape=[jax.ShapeDtypeStruct((exp_count, tok_rows, cols + lanes), BF16)] * 2,
        in_specs=[SMEM] + [VMEM] * 2,
        out_specs=[VMEM] * 2,
        compiler_params=pltpu.CompilerParams(vmem_limit_bytes=4 * MIB),
        name="piece",
    )(place, residual_in, marks)
    head_cols = context.shape[1]
    zeros = max(head_cols, cols + lanes)
    weight, done = fetch_weight(out_weight, [place, other, gains, picks], zeros)
    arrived = swap(other, "role", 1) + done[:, : cols + lanes]
    parted = [jnp.stack([mine[k], arrived[k]]) for k in range(exp_count)]
    near[0] = (context.reshape(-1, 8, head_cols) + done[:, :head_cols]).reshape(context.shape)

    gathered = [parted[0]] + [swap(parted[k], "exp", k) for k in range(1, exp_count)]
    blocks = []
    for value in near:
        blocks += [value, swap(value if blocks else context, "role", 1)]

    partial_sums = pl.pallas_call(
        functools.partial(project_kernel, tp_count, groups),
        out_shape=[jax.ShapeDtypeStruct((groups * tok_rows, cols), BF16)] * tp_count,
        in_specs=[SMEM] + [VMEM] * (groups + 1),
        out_specs=[VMEM] * tp_count,
        compiler_params=pltpu.CompilerParams(vmem_limit_bytes=(8 if groups <= 8 else 24) * MIB),
        name="project",
    )(place, *blocks, in_vmem([weight])[0])
    summands = [partial_sums[0]] + [swap(partial_sums[j], "tp", j) for j in range(1, tp_count)]

    gathered = jnp.stack(gathered).reshape(groups * tok_rows, cols + lanes)
    residual_cols = gathered[:, :cols]
    codes = gathered[:, cols].astype(jnp.int32)[None, :]

    places = [(q, side) for q in range(exp_count) for side in range(2)]
    ahead = near_steps
    up_block = fetch_up(
        places[2 * near_steps : 2 * near_steps + ahead], exp_count, cols, place, up_matrix, [partial_sums[0], gains, picks]
    )

    routed, after = [], up_block
    for steps in (range(near_steps), range(near_steps, exp_count)):
        kept, leaving = pl.pallas_call(
            functools.partial(slot_kernel, tp_count, exp_count, split, steps),
            out_shape=[jax.ShapeDtypeStruct((len(steps), slots, cols), BF16)] * 2,
            in_specs=[SMEM] + [VMEM] * (tp_count + 2) + [ANY],
            out_specs=[VMEM] * 2,
            compiler_params=pltpu.CompilerParams(
                vmem_limit_bytes=(6 if groups <= 8 else 24) * MIB
            ),
            name="slot",
        )(place, codes, residual_cols, *summands, after)
        arrived = swap(leaving, "role", 1)
        for at, q in enumerate(steps):
            both = jnp.stack([kept[at], arrived[at]])
            routed.append(swap(both, "exp", q) if q else both)
            after = both
    near_rows = jnp.stack(routed[:near_steps])
    far_rows = jnp.stack(routed[near_steps:])
    near_block = fetch_up(places[:1], exp_count, cols, place, up_matrix, [near_rows])
    near_all = [near_rows] + [swap(near_rows, "tp", j) for j in range(1, tp_count)]
    far_all = [far_rows] + [swap(far_rows, "tp", j) for j in range(1, tp_count)]

    rows = tp_count * slots
    small = rows <= 64
    half = near_steps * 2 * cols
    sums, squares, logits = pl.pallas_call(
        functools.partial(first_kernel, (tp_count, exp_count, split, near_steps)),
        out_shape=[
            pltpu.VMEM((rows, units), F32),
            pltpu.VMEM((rows, 128), F32),
            pltpu.VMEM((slots, 128), F32),
        ],
        in_specs=[SMEM] + [VMEM] * (3 + tp_count) + [HBM],
        out_specs=[VMEM] * 3,
        scratch_shapes=[
            pltpu.VMEM((rows, half), BF16),
            pltpu.VMEM((4, cols // 2, units), BF16),
            pltpu.SemaphoreType.DMA((4,)),
        ],
        compiler_params=pltpu.CompilerParams(vmem_limit_bytes=(14 if small else 36) * MIB),
        cost_estimate=pl.CostEstimate(
            flops=2 * rows * half * units, bytes_accessed=2 * half * units, transcendentals=0
        ),
        name="first",
    )(place, gains, router, *in_vmem([near_block]), *near_all, up_matrix)
    tile, depth = 256, 5
    early = width // cols * 5 // 8 * cols
    held = width // tile // 8 * tile
    sizes = (tp_count, exp_count, split, near_steps, far_steps, width, early)
    *early_outs, hidden, gate, held_block = pl.pallas_call(
        functools.partial(second_kernel, sizes),
        out_shape=[jax.ShapeDtypeStruct((slots, early), BF16)] * tp_count
        + [jax.ShapeDtypeStruct((rows, units), BF16), jax.ShapeDtypeStruct((slots, 128), F32)]
        + [pltpu.VMEM((units, held), BF16)],
        in_specs=[SMEM] + [VMEM] * (6 + tp_count) + [HBM] * 2,
        out_specs=[VMEM] * (tp_count + 3),
        scratch_shapes=[
            pltpu.VMEM((rows, width - half), BF16),
            pltpu.VMEM((rows, units), F32),
            pltpu.VMEM((4, cols // 2, units), BF16),
            pltpu.SemaphoreType.DMA((4,)),
            pltpu.VMEM((depth, units, tile), BF16),
            pltpu.SemaphoreType.DMA((depth,)),
            pltpu.SemaphoreType.DMA,
        ],
        compiler_params=pltpu.CompilerParams(vmem_limit_bytes=(22 if small else 40) * MIB),
        cost_estimate=pl.CostEstimate(
            flops=4 * rows * half * units, bytes_accessed=4 * half * units, transcendentals=0
        ),
        name="second",
    )(
        place, gains, router, *in_vmem([sums, squares, logits]), *far_all, *in_vmem([up_block]),
        up_matrix, down_matrix,
    )
    late_outs = pl.pallas_call(
        functools.partial(third_kernel, tp_count, early),
        out_shape=[jax.ShapeDtypeStruct((slots, width - early), BF16)] * tp_count,
        in_specs=[VMEM, VMEM, HBM],
        out_specs=[VMEM] * tp_count,
        scratch_shapes=[
            pltpu.VMEM((depth, units, tile), BF16),
            pltpu.SemaphoreType.DMA((depth,)),
        ],
        compiler_params=pltpu.CompilerParams(vmem_limit_bytes=(12 if small else 24) * MIB),
        cost_estimate=pl.CostEstimate(
            flops=2 * rows * half * units, bytes_accessed=2 * half * units, transcendentals=0
        ),
        name="third",
    )(hidden, *in_vmem([held_block]), down_matrix)

    early_sums = [early_outs[0]] + [swap(early_outs[j], "tp", j) for j in range(1, tp_count)]
    late_sums = [late_outs[0]] + [
        swap(late_outs[j] + 0 * early_sums[j][:, : width - early], "tp", j) for j in range(1, tp_count)
    ]
    all_rows = jnp.concatenate([near_rows, far_rows])
    home = ()
    for start, summands in ((0, early_sums), (early, late_sums)):
        size = summands[0].shape[1]
        home = pl.pallas_call(
            functools.partial(
                combine_kernel, tp_count, exp_count, split, start // cols, size
            ),
            out_shape=[jax.ShapeDtypeStruct((exp_count * CAP, width), BF16)] * 2,
            in_specs=[SMEM] + [VMEM] * (tp_count + 2 + len(home)),
            out_specs=[VMEM] * 2,
            input_output_aliases={tp_count + 3 + at: at for at in range(len(home))},
            compiler_params=pltpu.CompilerParams(vmem_limit_bytes=(8 if small else 40) * MIB),
            name="combine",
        )(place, all_rows, gate, *summands, *home)
    stay, leave = home
    back = swap(leave, "role", 1)
    pieces = []
    for q in range(exp_count):
        own = slice(q * CAP, (q + 1) * CAP)
        piece = jnp.concatenate([stay[own], back[own]])
        pieces.append(swap(piece, "exp", q) if q else piece)
    return pl.pallas_call(
        final_kernel,
        out_shape=jax.ShapeDtypeStruct((tok_rows, width), BF16),
        in_specs=[VMEM] * (1 + len(pieces)),
        out_specs=VMEM,
        compiler_params=pltpu.CompilerParams(vmem_limit_bytes=8 * MIB),
        name="final",
    )(picks, *pieces)


def solution(mesh):
    in_specs = (
        P(("role", "exp", "tp"), None),
        P(("role", "exp"), "tp"),
        P("tp", ("role", "exp")),
        P(),
        P(),
        P("role", "exp", None, "tp"),
        P("role", "exp", "tp", None),
        P(("role", "exp", "tp")),
        P(("role", "exp", "tp")),
    )
    out_specs = P(("role", "exp", "tp"), None)
    return jax.shard_map(
        per_device, mesh=mesh, in_specs=in_specs, out_specs=out_specs, check_vma=False
    )
```
